128 devices in a mesh: seq: 32 (over y, z, core), head: 4 (over x).
Axes of the slice: x: 4, y: 4, z: 4, core: 2. Of those that a mesh axis runs over, the one named last changes fastest.
Arguments:
- x_input: bfloat16 [32768, 8192], P('seq', 'head'), may hold values from -6 to 6
- z_input: bfloat16 [32768, 8192], P('seq', 'head'), may hold values from -6 to 6
- bc_input: bfloat16 [32768, 8, 256], P('seq', 'head'), may hold values from -6 to 6
- conv_weight_x: float32 [4, 8192], P(None, 'head'), may hold values from -3 to 3
- conv_weight_bc: float32 [4, 8, 256], P(None, 'head'), may hold values from -3 to 3
- step_size: float32 [32768, 128], P('seq', 'head'), may hold values from 0 to 1
- log_decay: float32 [32768, 128], P('seq', 'head'), may hold values from -1 to 0
- skip_gain: float32 [128], P('head'), may hold values from 0.5 to 2
- norm_gain: float32 [8192], P('head'), may hold values from 0.1 to 1.9
- out_weight: bfloat16 [8192, 4096], P('head'), may hold values from -0.0625 to 0.0625
Outputs:
- layer_out: bfloat16 [32768, 4096], P(('seq', 'head'))
The draws below stay inside these ranges and needn't reach their ends.
All inputs are finite; a program needn't handle non-finite values.
Results may differ from the reference program's by a relative error of at most 0.012.
Values may be sent and summed in bfloat16 or wider, within the bound.
A program may use at most 256 MiB of HBM per device.

```python
import math
import jax
import jax.numpy as jnp
from jax import lax

D = 4096
H = 128
P_SIZE = 64
N = 128
G = 8
KCONV = 4
BLOCK_LEN = 256
TOK_DEV = 1024
DI = 8192
TEXT_ITEMS = 32768


def head_rates(key):
    seq_devices = TEXT_ITEMS // TOK_DEV
    stochastic_seeds = jax.random.split(jax.random.fold_in(key, 11), 3)
    fast_share = 0.15
    spectrum_top = 3.0
    spectrum_low = 0.03 / seq_devices
    fast_heads = jax.random.uniform(stochastic_seeds[0], (H,), jnp.float32) < fast_share
    fast_low = math.log(max(TOK_DEV / 50.0, 3.0))
    fast_high = math.log(max(TOK_DEV / 30.0, 5.0))
    fast_device = jnp.exp(jax.random.uniform(stochastic_seeds[1], (H,), jnp.float32, fast_low, fast_high))
    spread_device = jnp.exp(jax.random.uniform(stochastic_seeds[2], (H,), jnp.float32, math.log(spectrum_low), math.log(spectrum_top)))
    return jnp.where(fast_heads, fast_device, spread_device) / TOK_DEV


def device_blocks(key):
    seq_devices = TEXT_ITEMS // TOK_DEV
    factor = jnp.exp(jax.random.uniform(key, (seq_devices, 1, H), jnp.float32, math.log(0.5), math.log(2.0)))
    return jnp.broadcast_to(factor, (seq_devices, TOK_DEV, H)).reshape(TEXT_ITEMS, H)


def draw_log_decay(key, part):
    forgetting_speeds = head_rates(key)
    stochastic_seeds = jax.random.split(jax.random.fold_in(key, 21), 4)
    seed_shift_amount = jax.random.uniform(stochastic_seeds[0], (TEXT_ITEMS, H), jnp.float32, 0.5, 1.5)
    processor_factor = device_blocks(stochastic_seeds[1])
    segment_entries = jax.random.randint(stochastic_seeds[2], (2,), 0, TEXT_ITEMS)
    segment_span = jax.random.uniform(stochastic_seeds[3], (2,), jnp.float32, 0.22, 0.45)
    symbol_indices = jnp.arange(TEXT_ITEMS)
    symbol_segment = jnp.sum(jnp.where(symbol_indices[:, None] == segment_entries[None, :], segment_span[None, :], 0.0), axis=1)
    return -jnp.minimum(forgetting_speeds[None, :] * seed_shift_amount * processor_factor + symbol_segment[:, None], 1.0)


def draw_step_size(key, part):
    forgetting_speeds = head_rates(key)
    stochastic_seeds = jax.random.split(jax.random.fold_in(key, 31), 2)
    seed_shift_amount = jnp.exp(jax.random.uniform(stochastic_seeds[0], (TEXT_ITEMS, H), jnp.float32, math.log(0.5), math.log(2.0)))
    processor_factor = device_blocks(stochastic_seeds[1])
    floor_rate = jnp.maximum(forgetting_speeds, 1.0 / TEXT_ITEMS)
    return jnp.minimum(2.0 * floor_rate[None, :] * seed_shift_amount * processor_factor, 1.0)


def levels(own_key, dims, shards, smallest, largest):
    gain = 1.0
    for dim, blocks in shards:
        draws = jax.random.uniform(jax.random.fold_in(jax.random.fold_in(own_key, 6), dim), (blocks,), jnp.float32, smallest / len(shards), largest / len(shards))
        gain = gain * jnp.repeat(jnp.exp(draws), dims[dim] // blocks).reshape((-1,) + (1,) * (len(dims) - 1 - dim))
    return gain


def centred(own_key, shape, width, reach, shards=(), kind=jnp.bfloat16):
    result = width * jax.random.normal(own_key, shape, jnp.float32)
    if shards:
        result = result * levels(own_key, shape, shards, -0.22, 0.18)
    return jnp.clip(result, -reach, reach).astype(kind)


def setup_inputs(seed: int = 0) -> dict:
    arg_keys = jax.random.split(jax.random.key(seed), 11)
    return {
        "x_input": centred(arg_keys[0], (TEXT_ITEMS, DI), 1.0, 6.0, ((0, 32), (1, 4))),
        "z_input": centred(arg_keys[1], (TEXT_ITEMS, DI), 1.0, 6.0, ((0, 32), (1, 4))),
        "bc_input": centred(arg_keys[2], (TEXT_ITEMS, G, 2 * N), 1.0, 6.0, ((0, 32), (1, 4))),
        "conv_weight_x": centred(arg_keys[3], (KCONV, DI), 0.5, 3.0, ((1, 4),), jnp.float32),
        "conv_weight_bc": centred(arg_keys[4], (KCONV, G, 2 * N), 0.5, 3.0, ((1, 4),), jnp.float32),
        "step_size": draw_step_size(jax.random.fold_in(arg_keys[10], 71), 0),
        "log_decay": draw_log_decay(jax.random.fold_in(arg_keys[10], 71), 0),
        "skip_gain": jnp.clip(jnp.exp(math.log(2.0) - 1.3862944 * jax.random.uniform(arg_keys[7], (H,), jnp.float32) ** levels(arg_keys[7], (H,), ((0, 4),), -0.2, 0.2)), 0.5, 2.0),
        "norm_gain": jnp.clip(1.0 + 0.18 * jax.random.normal(arg_keys[8], (DI,), jnp.float32), 0.1, 1.9),
        "out_weight": centred(arg_keys[9], (DI, D), DI ** -0.5, 0.0625, ((0, 4),)),
    }


EPS = 1e-05

def conv_silu(padded, weight, length):
    summed = jnp.zeros((length,) + padded.shape[1:], jnp.float32)
    for offset in range(weight.shape[0]):
        summed = summed + weight[offset] * padded[offset:offset + length].astype(jnp.float32)
    return jax.nn.silu(summed).astype(jnp.bfloat16)

def reference(x_input, z_input, bc_input, conv_weight_x, conv_weight_bc, step_size, log_decay, skip_gain, norm_gain, out_weight):
    lead_rows = KCONV - 1
    x_conv = conv_silu(jnp.concatenate([jnp.zeros((lead_rows, DI), jnp.bfloat16), x_input], 0), conv_weight_x, TEXT_ITEMS)
    bc_conv = conv_silu(jnp.concatenate([jnp.zeros((lead_rows, G, 2 * N), jnp.bfloat16), bc_input], 0), conv_weight_bc, TEXT_ITEMS)
    per_group = H // G
    blocks = TEXT_ITEMS // BLOCK_LEN
    highest = lax.Precision.HIGHEST
    lower_mask = jnp.tril(jnp.ones((BLOCK_LEN, BLOCK_LEN), bool))[:, :, None, None]
    skip_table = skip_gain.reshape(G, per_group)

    def advance(carry_state, block_data):
        x_block, bc_block, step_block, decay_block, z_block = block_data
        x_float = x_block.astype(jnp.float32).reshape(BLOCK_LEN, G, per_group, P_SIZE)
        bc_float = bc_block.astype(jnp.float32)
        b_mat = bc_float[..., :N]
        c_mat = bc_float[..., N:]
        driven = step_block.reshape(BLOCK_LEN, G, per_group)[..., None] * x_float
        cumulative = jnp.cumsum(decay_block.reshape(BLOCK_LEN, G, per_group), axis=0)
        log_gap = cumulative[:, None] - cumulative[None, :]
        decay_table = jnp.where(lower_mask, jnp.exp(jnp.where(lower_mask, log_gap, 0.0)), 0.0)
        scores = jnp.einsum('tgn,sgn->tsg', c_mat, b_mat, precision=highest)
        within = jnp.einsum('tsgh,sghp->tghp', scores[..., None] * decay_table, driven, precision=highest)
        carried = jnp.exp(cumulative)[..., None] * jnp.einsum('tgn,ghnp->tghp', c_mat, carry_state, precision=highest)
        mixed = within + carried + skip_table[..., None] * x_float
        last_log = cumulative[-1]
        fading = jnp.exp(last_log[None] - cumulative)[..., None] * driven
        carry_state = jnp.exp(last_log)[..., None, None] * carry_state + jnp.einsum('sgn,sghp->ghnp', b_mat, fading, precision=highest)
        gated_out = mixed.reshape(BLOCK_LEN, DI) * jax.nn.silu(z_block.astype(jnp.float32))
        grouped = gated_out.reshape(BLOCK_LEN, G, DI // G)
        normed = grouped * lax.rsqrt(lax.optimization_barrier(jnp.mean(grouped * grouped, axis=-1, keepdims=True)) + EPS)
        normed = (normed.reshape(BLOCK_LEN, DI) * norm_gain).astype(jnp.bfloat16)
        return (carry_state, jnp.dot(normed, out_weight, preferred_element_type=jnp.float32).astype(jnp.bfloat16))
    inputs = (x_conv.reshape(blocks, BLOCK_LEN, DI), bc_conv.reshape(blocks, BLOCK_LEN, G, 2 * N), step_size.reshape(blocks, BLOCK_LEN, H), log_decay.reshape(blocks, BLOCK_LEN, H), z_input.reshape(blocks, BLOCK_LEN, DI))
    initial = jnp.zeros((G, per_group, N, P_SIZE), jnp.float32)
    _, outputs = lax.scan(advance, initial, inputs)
    return outputs.reshape(TEXT_ITEMS, D)
```

```python
import functools

import jax
import jax.numpy as jnp
from jax import lax
from jax.experimental import pallas as pl
from jax.experimental.pallas import tpu as pltpu
from jax.sharding import PartitionSpec as P

P_SIZE = 64
N = 128
KCONV = 4
EPS = 1e-05
Q = 128
LEAD = 16
TILE = 256
PIECES = 4
HEADS = 4

MESH = pl.DeviceIdType.MESH
F32 = jnp.float32
BF16 = jnp.bfloat16


def split3(value):
    hi = value.astype(BF16)
    rest = value - hi.astype(F32)
    mid = rest.astype(BF16)
    return hi, mid, (rest - mid.astype(F32)).astype(BF16)


def dot(a, b):
    return jnp.dot(a, b, preferred_element_type=F32)


def silu(v):
    return v * (0.5 * jnp.tanh(0.5 * v) + 0.5)


def kernel(
    ns,
    x_hbm,
    z_hbm,
    bc_hbm,
    w_hbm,
    cwx,
    cwbc,
    step_ref,
    ld_ref,
    skip_ref,
    gain_ref,
    out_hbm,
    xb,
    zb,
    bcb,
    wb,
    ub,
    pst,
    fac,
    e4,
    a4,
    u4,
    em,
    et,
    eo,
    rt,
    skx,
    dl_all,
    dexp,
    fmsg,
    frecv,
    imsg,
    irecv,
    gbuf,
    rs_send,
    rs_recv,
    local_sem,
    halo_send,
    halo_recv,
    dl_s,
    dl_r,
    f_s,
    f_r,
    i_s,
    i_r,
    r_s,
    r_r,
    out_sem,
):
    length, width = x_hbm.shape
    columns = w_hbm.shape[1]
    heads = step_ref.shape[1]
    groups = bc_hbm.shape[1] // (2 * N)
    gw = width // groups
    blocks = length // Q
    chunk_rows = length // HEADS
    half = columns // 2
    piece = half // PIECES
    row_parts = N // 16
    col_parts = ns // row_parts
    part = width // col_parts

    me = lax.axis_index("seq")
    d = lax.axis_index("head")
    right = lax.rem(d + 1, HEADS)
    left = lax.rem(d + HEADS - 1, HEADS)
    after = lax.rem(me + 1, ns)

    barrier = pltpu.get_barrier_semaphore()

    def greet(k, carry):
        pl.semaphore_signal(barrier, inc=1, device_id=(lax.rem(me + k, ns), d), device_id_type=MESH)
        return carry

    lax.fori_loop(1, ns, greet, 0)
    for other in (right, left):
        pl.semaphore_signal(barrier, inc=1, device_id=(me, other), device_id_type=MESH)

    def load_x(g):
        return pltpu.make_async_copy(
            x_hbm.at[:, pl.ds(g * gw, gw)],
            xb.at[pl.ds(LEAD, length), pl.ds(g * gw, gw)],
            local_sem.at[g],
        )

    load_bc = pltpu.make_async_copy(bc_hbm, bcb.at[pl.ds(LEAD, length)], local_sem.at[2])
    load_z = pltpu.make_async_copy(z_hbm, zb, local_sem.at[3])

    def load_w(h):
        return pltpu.make_async_copy(
            w_hbm.at[:, pl.ds(h * half, half)], wb.at[:, pl.ds(h * half, half)], local_sem.at[4 + h]
        )

    load_bc.start()
    load_x(0).start()
    load_x(1).start()

    lanes = 128
    lane_row = lax.broadcasted_iota(jnp.int32, (lanes, TILE), 0)
    lane_col = lax.broadcasted_iota(jnp.int32, (lanes, TILE), 1)
    for tile in range(width // TILE):
        head = lax.div(lane_col + tile * TILE, P_SIZE)
        spread = (head == lax.rem(lane_row, heads)) & (lane_row < 3 * heads)
        e4[:, tile * TILE : (tile + 1) * TILE] = jnp.where(spread, 1.0, 0.0).astype(BF16)

    def pack(value):
        hi, mid, lo = split3(value)
        lane = lax.broadcasted_iota(jnp.int32, value.shape, 1)
        hi, mid, lo = hi.astype(F32), mid.astype(F32), lo.astype(F32)
        chosen = jnp.where(lane < heads, hi, jnp.where(lane < 2 * heads, mid, lo))
        return jnp.where(lane < 3 * heads, chosen, 0.0).astype(BF16)

    rep = jnp.where(
        lax.rem(lax.broadcasted_iota(jnp.int32, (heads, lanes), 1), heads)
        == lax.broadcasted_iota(jnp.int32, (heads, lanes), 0),
        1.0,
        0.0,
    ).astype(BF16)
    low = jnp.where(
        lax.broadcasted_iota(jnp.int32, (Q, Q), 0) >= lax.broadcasted_iota(jnp.int32, (Q, Q), 1), 1.0, 0.0
    ).astype(BF16)

    def exact(left_mat, parts):
        return dot(left_mat, parts[0]) + dot(left_mat, parts[1]) + dot(left_mat, parts[2])

    mids, tots = [], []
    for b in range(blocks):
        rows = slice(b * Q, (b + 1) * Q)
        parts = split3(ld_ref[rows, :])
        ld4 = dot(parts[0], rep) + dot(parts[1], rep) + dot(parts[2], rep)
        parts = split3(step_ref[rows, :])
        step4 = dot(parts[0], rep) + dot(parts[1], rep) + dot(parts[2], rep)
        cum = exact(low, split3(ld4))
        mid = cum[Q // 2 - 1 : Q // 2, :]
        a4[rows, :] = pack(jnp.exp(cum - mid))
        u4[rows, :] = pack(step4 * jnp.exp(mid - cum))
        mids.append(mid)
        tots.append(cum[Q - 1 : Q, :])
    row = lax.broadcasted_iota(jnp.int32, (blocks, lanes), 0)
    zero = jnp.zeros((blocks, lanes), F32)
    m8, t8, o8, s8 = zero, zero, zero, zero
    run = jnp.zeros((1, lanes), F32)
    for b in range(blocks):
        m8 = jnp.where(row == b, mids[b], m8)
        t8 = jnp.where(row == b, tots[b], t8)
        o8 = jnp.where(row == b, run, o8)
        run = run + tots[b]
    dl_all[me] = jnp.broadcast_to(run, (8, lanes))
    later = jnp.zeros((1, lanes), F32)
    for b in reversed(range(blocks)):
        s8 = jnp.where(row == b, later, s8)
        later = later + tots[b]

    pl.semaphore_wait(barrier, ns + 1)

    def halo(kind, src, dst):
        return pltpu.make_async_remote_copy(
            src_ref=src.at[pl.ds(length - LEAD, LEAD)],
            dst_ref=dst.at[pl.ds(0, LEAD)],
            send_sem=halo_send.at[kind],
            recv_sem=halo_recv.at[kind],
            device_id=(after, d),
            device_id_type=MESH,
        )

    halo(0, x_hbm, xb).start()
    halo(1, bc_hbm, bcb).start()

    def to_seq(src, dst, send, recv, slot, there, other):
        return pltpu.make_async_remote_copy(
            src_ref=src.at[slot],
            dst_ref=dst.at[there],
            send_sem=send.at[slot],
            recv_sem=recv.at[there],
            device_id=(other, d),
            device_id_type=MESH,
        )

    def decay_copy(j):
        return pltpu.make_async_remote_copy(
            src_ref=dl_all.at[me],
            dst_ref=dl_all.at[me],
            send_sem=dl_s.at[j],
            recv_sem=dl_r.at[me],
            device_id=(j, d),
            device_id_type=MESH,
        )

    def send_decay(k, carry):
        decay_copy(lax.rem(me + k, ns)).start()
        return carry

    lax.fori_loop(1, ns, send_decay, 0)

    for ref, value in (
        (em, jnp.exp(m8)),
        (et, jnp.exp(t8 - m8)),
        (eo, jnp.exp(o8)),
        (rt, jnp.exp(s8 + t8 - m8)),
    ):
        ref[...] = dot(pack(value), e4[...])
    parts = split3(jnp.broadcast_to(skip_ref[...], (8, heads)))
    skx[...] = dot(pack(dot(parts[0], rep) + dot(parts[1], rep) + dot(parts[2], rep)), e4[...])

    def conv(buf, weight, r0, cols):
        prev = buf[pl.ds(r0, LEAD), cols].astype(F32)[LEAD - 8 :]
        cur = buf[pl.ds(r0 + LEAD, Q), cols].astype(F32)
        ext = jnp.concatenate([prev, cur], 0)
        total = weight[KCONV - 1 : KCONV, cols] * cur
        for k in range(1, KCONV):
            total = total + weight[KCONV - 1 - k : KCONV - k, cols] * pltpu.roll(ext, k, 0)[8:]
        done = silu(total).astype(BF16)
        buf[pl.ds(r0 + LEAD, Q), cols] = done
        return done

    load_bc.wait()
    for g in range(groups):
        load_x(g).wait()
        if g == groups - 1:
            load_z.start()
            load_w(0).start()
            load_w(1).start()

        def first_pass(turn, carry, g=g):
            b = blocks - 1 - turn
            r0 = pl.multiple_of(b * Q, Q)

            if g == 0:

                @pl.when(b == 0)
                def _():
                    halo(0, x_hbm, xb).wait_recv()
                    halo(1, bc_hbm, bcb).wait_recv()

                    @pl.when(me == 0)
                    def _():
                        xb[:LEAD, :] = jnp.zeros((LEAD, width), BF16)
                        bcb[:LEAD, :] = jnp.zeros((LEAD, bcb.shape[1]), BF16)

            bc = conv(bcb, cwbc, r0, slice(g * 2 * N, (g + 1) * 2 * N))
            b_turned = bc[:, :N].astype(F32).T.astype(BF16)
            for tile in range(gw // TILE):
                cols = slice(g * gw + tile * TILE, g * gw + (tile + 1) * TILE)
                xc = conv(xb, cwx, r0, cols).astype(F32)
                u = (xc * dot(u4[pl.ds(r0, Q), :], e4[:, cols])).astype(BF16)
                ub[pl.ds(r0, Q), cols] = u
                fresh = dot(b_turned, u)
                pst[b, :, cols] = fresh
                scaled = rt[pl.ds(b, 1), cols] * fresh
                fac[:, cols] = jnp.where(turn == 0, scaled, fac[:, cols] + scaled)
            return carry

        lax.fori_loop(0, blocks, first_pass, 0)
        for rp in range(row_parts):
            for cp in range(g * col_parts // groups, (g + 1) * col_parts // groups):
                fmsg[rp * col_parts + cp] = fac[
                    rp * 16 : (rp + 1) * 16, cp * part : (cp + 1) * part
                ].astype(BF16)

        def send_state(k, carry, g=g):
            j = lax.rem(me + k, ns)

            @pl.when(lax.div(lax.rem(j, col_parts), col_parts // groups) == g)
            def _():
                to_seq(fmsg, frecv, f_s, f_r, j, me, j).start()

            return carry

        lax.fori_loop(1, ns, send_state, 0)

    def recur(tile, carry):
        cols = pl.ds(pl.multiple_of(tile * 128, 128), 128)
        state = jnp.zeros((N, 128), F32)
        for b in range(blocks):
            fresh = pst[b, :, cols]
            pst[b, :, cols] = state
            state = et[b : b + 1, cols] * (fresh + em[b : b + 1, cols] * state)
        return carry

    lax.fori_loop(0, width // 128, recur, 0)

    def await_decay(k, carry):
        j = lax.rem(me + k, ns)
        pltpu.make_async_remote_copy(
            src_ref=dl_all.at[j],
            dst_ref=dl_all.at[j],
            send_sem=dl_s.at[j],
            recv_sem=dl_r.at[j],
            device_id=(j, d),
            device_id_type=MESH,
        ).wait_recv()
        return carry

    lax.fori_loop(1, ns, await_decay, 0)
    mine = pl.multiple_of(lax.rem(me, col_parts) * part, part)
    dexp[...] = dot(
        pack(jnp.exp(dl_all[...].reshape(ns * 8, lanes))), e4[:, pl.ds(mine, part)]
    )
    frecv[me] = fmsg[me]

    def relay(i, state):
        @pl.when(i != me)
        def _():
            to_seq(fmsg, frecv, f_s, f_r, i, i, i).wait_recv()

        imsg[i] = state.astype(BF16)

        @pl.when(i != me)
        def _():
            to_seq(imsg, irecv, i_s, i_r, i, me, i).start()

        fade = dexp[pl.ds(pl.multiple_of(i * 8, 8), 8), :]
        return jnp.concatenate([fade, fade], 0) * state + frecv[i].astype(F32)

    lax.fori_loop(0, ns, relay, jnp.zeros((16, part), F32))
    irecv[me] = imsg[me]

    def await_state(k, carry):
        j = lax.rem(me + k, ns)
        to_seq(imsg, irecv, i_s, i_r, j, j, j).wait_recv()
        return carry

    lax.fori_loop(1, ns, await_state, 0)
    for rp in range(row_parts):
        for cp in range(col_parts):
            fac[rp * 16 : (rp + 1) * 16, cp * part : (cp + 1) * part] = irecv[
                rp * col_parts + cp
            ].astype(F32)
    load_z.wait()

    mask = lax.broadcasted_iota(jnp.int32, (Q, Q), 0) >= lax.broadcasted_iota(jnp.int32, (Q, Q), 1)

    def second_pass(chunk):
        def one(i, carry):
            b = chunk * (chunk_rows // Q) + i
            r0 = pl.multiple_of(b * Q, Q)
            for g in range(groups):
                b_mat = bcb[pl.ds(r0 + LEAD, Q), g * 2 * N : g * 2 * N + N]
                c_mat = bcb[pl.ds(r0 + LEAD, Q), g * 2 * N + N : (g + 1) * 2 * N]
                scores = lax.dot_general(
                    c_mat, b_mat, (((1,), (1,)), ((), ())), preferred_element_type=F32
                )
                lhs = jnp.concatenate([jnp.where(mask, scores, 0.0).astype(BF16), c_mat], 1)
                squares = jnp.zeros((Q, 128), F32)
                for tile in range(gw // TILE):
                    cols = slice(g * gw + tile * TILE, g * gw + (tile + 1) * TILE)
                    entering = em[pl.ds(b, 1), cols] * (
                        pst[b, :, cols] + eo[pl.ds(b, 1), cols] * fac[:, cols]
                    )
                    rhs = jnp.concatenate([ub[pl.ds(r0, Q), cols], entering.astype(BF16)], 0)
                    y = dot(a4[pl.ds(r0, Q), :], e4[:, cols]) * dot(lhs, rhs)
                    y = y + skx[0:1, cols] * xb[pl.ds(r0 + LEAD, Q), cols].astype(F32)
                    gated = y * silu(zb[pl.ds(r0, Q), cols].astype(F32))
                    gbuf[:, tile * TILE : (tile + 1) * TILE] = gated
                    for k in range(TILE // 128):
                        squares = squares + gated[:, k * 128 : (k + 1) * 128] ** 2
                mean = jnp.sum(squares, axis=1, keepdims=True) * (1.0 / gw)
                scale = lax.rsqrt(mean + EPS)
                for tile in range(gw // TILE):
                    cols = slice(g * gw + tile * TILE, g * gw + (tile + 1) * TILE)
                    ub[pl.ds(r0, Q), cols] = (
                        gbuf[:, tile * TILE : (tile + 1) * TILE] * scale * gain_ref[:, cols]
                    ).astype(BF16)
            return carry

        lax.fori_loop(0, chunk_rows // Q, one, 0)

    def product(way, p, chunk):
        first = pl.multiple_of(way * half + p * piece, piece)
        rows = pl.ds(pl.multiple_of(chunk * chunk_rows, chunk_rows), chunk_rows)
        return dot(ub[rows, :], wb[:, pl.ds(first, piece)])

    def hop(way, turn, p):
        return pltpu.make_async_remote_copy(
            src_ref=rs_send.at[way, turn, p],
            dst_ref=rs_recv.at[way, turn, p],
            send_sem=r_s.at[way, turn, p],
            recv_sem=r_r.at[way, turn, p],
            device_id=(me, jnp.where(way == 0, right, left)),
            device_id_type=MESH,
        )

    def stage(way, turn, p):
        chunk = lax.rem(jnp.where(way == 0, d + 2 * HEADS - 1 - turn, d + 1 + turn), HEADS)
        total = product(way, p, chunk)
        if turn > 0:
            hop(way, turn - 1, p).wait_recv()
            total = total + rs_recv[way, turn - 1, p].astype(F32)
        rs_send[way, turn, p] = total.astype(BF16)
        hop(way, turn, p).start()

    def first_stages(k, carry):
        second_pass(lax.rem(jnp.where(k == 0, left, right), HEADS))

        def run_piece(p, inner):
            stage(k, 0, p)
            return inner

        lax.fori_loop(0, PIECES, run_piece, 0)
        return carry

    def both(turn):
        def run_piece(q, carry):
            stage(lax.rem(q, 2), turn, lax.div(q, 2))
            return carry

        lax.fori_loop(0, 2 * PIECES, run_piece, 0)

    load_w(0).wait()
    load_w(1).wait()
    lax.fori_loop(0, 2, first_stages, 0)
    second_pass(lax.rem(d + 2, HEADS))
    both(1)
    second_pass(d)
    both(2)

    def own(q, carry):
        total = product(lax.rem(q, 2), lax.div(q, 2), d)
        pst[q, :, 0:piece] = total[:Q]
        pst[q, :, piece : 2 * piece] = total[Q:]
        return carry

    lax.fori_loop(0, 2 * PIECES, own, 0)

    def to_out(way, p):
        first = pl.multiple_of(way * half + p * piece, piece)
        return pltpu.make_async_copy(
            zb.at[
                pl.ds(pl.multiple_of(way * chunk_rows, chunk_rows), chunk_rows),
                pl.ds(pl.multiple_of(p * piece, piece), piece),
            ],
            out_hbm.at[:, pl.ds(first, piece)],
            out_sem.at[way, p],
        )

    def finish(q, carry):
        way, p = lax.rem(q, 2), lax.div(q, 2)
        hop(way, HEADS - 2, p).wait_recv()
        arrived = rs_recv[way, HEADS - 2, p].astype(F32)
        cols = pl.ds(pl.multiple_of(p * piece, piece), piece)
        base = pl.multiple_of(way * chunk_rows, chunk_rows)
        zb[pl.ds(base, Q), cols] = (pst[q, :, 0:piece] + arrived[:Q]).astype(BF16)
        zb[pl.ds(base + Q, Q), cols] = (pst[q, :, piece : 2 * piece] + arrived[Q:]).astype(BF16)
        to_out(way, p).start()
        return carry

    lax.fori_loop(0, 2 * PIECES, finish, 0)

    halo(0, x_hbm, xb).wait_send()
    halo(1, bc_hbm, bcb).wait_send()

    def await_sends(k, carry):
        j = lax.rem(me + k, ns)
        decay_copy(j).wait_send()
        to_seq(fmsg, frecv, f_s, f_r, j, me, j).wait_send()
        to_seq(imsg, irecv, i_s, i_r, j, me, j).wait_send()
        return carry

    lax.fori_loop(1, ns, await_sends, 0)

    def await_ring(q, carry):
        way, p = lax.rem(q, 2), lax.div(q, 2)
        for turn in range(HEADS - 1):
            hop(way, turn, p).wait_send()
        to_out(way, p).wait()
        return carry

    lax.fori_loop(0, 2 * PIECES, await_ring, 0)


def local(
    x_input,
    z_input,
    bc_input,
    conv_weight_x,
    conv_weight_bc,
    step_size,
    log_decay,
    skip_gain,
    norm_gain,
    out_weight,
):
    ns = lax.axis_size("seq")
    length, width = x_input.shape
    groups = bc_input.shape[1]
    columns = out_weight.shape[1]
    blocks = length // Q
    heads = step_size.shape[1]
    part = width // (ns // (N // 16))
    piece = columns // 2 // PIECES
    rows = length // HEADS
    any_space = pl.BlockSpec(memory_space=pl.ANY)
    vmem = pl.BlockSpec(memory_space=pltpu.VMEM)
    dma = pltpu.SemaphoreType.DMA
    return pl.pallas_call(
        functools.partial(kernel, ns),
        out_shape=jax.ShapeDtypeStruct((rows, columns), BF16),
        in_specs=[any_space] * 4 + [vmem] * 6,
        out_specs=any_space,
        scratch_shapes=[
            pltpu.VMEM((LEAD + length, width), BF16),
            pltpu.VMEM((length, width), BF16),
            pltpu.VMEM((LEAD + length, groups * 2 * N), BF16),
            pltpu.VMEM((width, columns), BF16),
            pltpu.VMEM((length, width), BF16),
            pltpu.VMEM((blocks, N, width), F32),
            pltpu.VMEM((N, width), F32),
            pltpu.VMEM((128, width), BF16),
            pltpu.VMEM((length, 128), BF16),
            pltpu.VMEM((length, 128), BF16),
            pltpu.VMEM((blocks, width), F32),
            pltpu.VMEM((blocks, width), F32),
            pltpu.VMEM((blocks, width), F32),
            pltpu.VMEM((blocks, width), F32),
            pltpu.VMEM((8, width), F32),
            pltpu.VMEM((ns, 8, 128), F32),
            pltpu.VMEM((ns * 8, part), F32),
            pltpu.VMEM((ns, 16, part), BF16),
            pltpu.VMEM((ns, 16, part), BF16),
            pltpu.VMEM((ns, 16, part), BF16),
            pltpu.VMEM((ns, 16, part), BF16),
            pltpu.VMEM((Q, width // groups), F32),
            pltpu.VMEM((2, HEADS - 1, PIECES, rows, piece), BF16),
            pltpu.VMEM((2, HEADS - 1, PIECES, rows, piece), BF16),
            dma((6,)),
            dma((2,)),
            dma((2,)),
            dma((ns,)),
            dma((ns,)),
            dma((ns,)),
            dma((ns,)),
            dma((ns,)),
            dma((ns,)),
            dma((2, HEADS - 1, PIECES)),
            dma((2, HEADS - 1, PIECES)),
            dma((2, PIECES)),
        ],
        compiler_params=pltpu.CompilerParams(
            collective_id=0, has_side_effects=True, vmem_limit_bytes=60 * 2**20
        ),
        cost_estimate=pl.CostEstimate(
            flops=2 * length * width * columns,
            bytes_accessed=2 * (2 * length * width + width * columns),
            transcendentals=2 * length * width,
        ),
    )(
        x_input,
        z_input,
        bc_input.reshape(length, groups * 2 * N),
        out_weight,
        conv_weight_x,
        conv_weight_bc.reshape(KCONV, groups * 2 * N),
        step_size,
        log_decay,
        skip_gain.reshape(1, heads),
        norm_gain.reshape(1, width),
    )


def solution(mesh):
    in_specs = (
        P("seq", "head"),
        P("seq", "head"),
        P("seq", "head", None),
        P(None, "head"),
        P(None, "head", None),
        P("seq", "head"),
        P("seq", "head"),
        P("head"),
        P("head"),
        P("head", None),
    )
    out_specs = P(("seq", "head"), None)
    return jax.shard_map(local, mesh=mesh, in_specs=in_specs, out_specs=out_specs, check_vma=False)
```

```python
import functools

import jax
import jax.numpy as jnp
from jax import lax
from jax.experimental import pallas as pl
from jax.experimental.pallas import tpu as pltpu
from jax.sharding import PartitionSpec as P

P_SIZE = 64
N = 128
KCONV = 4
EPS = 1e-05
Q = 128
LEAD = 16
TILE = 256
CONV_COLS = 256
PIECES = 4
HEADS = 4

MESH = pl.DeviceIdType.MESH
F32 = jnp.float32
BF16 = jnp.bfloat16


def split3(value):
    hi = value.astype(BF16)
    rest = value - hi.astype(F32)
    mid = rest.astype(BF16)
    return hi, mid, (rest - mid.astype(F32)).astype(BF16)


def dot(a, b):
    return jnp.dot(a, b, preferred_element_type=F32)


def kernel(
    ns,
    x_hbm,
    z_hbm,
    bc_hbm,
    w_hbm,
    cwx,
    cwbc,
    step_ref,
    ld_ref,
    skip_ref,
    gain_ref,
    out_hbm,
    xb,
    zb,
    bcr,
    bcb,
    wb,
    ub,
    pst,
    fac,
    e4,
    a4,
    u4,
    em,
    et,
    eo,
    rt,
    skx,
    taps_x,
    taps_bc,
    dl_pair,
    pair_send,
    pair_recv,
    fmsg,
    frecv,
    imsg,
    irecv,
    gbuf,
    rs_send,
    rs_recv,
    local_sem,
    halo_send,
    halo_recv,
    pair_s,
    pair_r,
    f_s,
    f_r,
    i_s,
    i_r,
    r_s,
    r_r,
    out_sem,
):
    length, width = x_hbm.shape
    columns = w_hbm.shape[1]
    heads = step_ref.shape[0]
    groups = bc_hbm.shape[1] // (2 * N)
    gw = width // groups
    blocks = length // Q
    chunk_rows = length // HEADS
    half = columns // 2
    piece = half // PIECES
    chips = ns // 2
    row_parts = N // 16
    col_parts = chips // row_parts
    part = gw // col_parts
    strip = LEAD + length
    strips = width // piece

    me = lax.axis_index("seq")
    d = lax.axis_index("head")
    right = lax.rem(d + 1, HEADS)
    left = lax.rem(d + HEADS - 1, HEADS)
    after = lax.rem(me + 1, ns)
    chip, core = lax.div(me, 2), lax.rem(me, 2)
    sibling = me + 1 - 2 * core

    barrier = pltpu.get_barrier_semaphore()

    def load_x(q):
        return pltpu.make_async_copy(
            x_hbm.at[:, pl.ds(pl.multiple_of(q * piece, piece), piece)],
            rs_send.at[pl.ds(pl.multiple_of(q * strip + LEAD, LEAD), length)],
            local_sem.at[q],
        )

    load_bc = pltpu.make_async_copy(bc_hbm, bcr.at[pl.ds(LEAD, length)], local_sem.at[strips])
    load_z = pltpu.make_async_copy(z_hbm, zb, local_sem.at[strips + 1])

    def load_w(h):
        return pltpu.make_async_copy(
            w_hbm.at[:, pl.ds(h * half, half)],
            wb.at[:, pl.ds(h * half, half)],
            local_sem.at[strips + 2 + h],
        )

    load_bc.start()
    per_group = strips // groups
    for q in range(per_group):
        load_x((1 - core) * per_group + q).start()
    for q in range(per_group):
        load_x(core * per_group + q).start()

    def greet(k, carry):
        other = 2 * lax.rem(chip + k, chips) + core
        pl.semaphore_signal(barrier, inc=1, device_id=(other, d), device_id_type=MESH)
        return carry

    lax.fori_loop(1, chips, greet, 0)
    across = lax.rem(jnp.where(core == 0, me + ns - 1, me + 1), ns)
    for other in (sibling, across):
        pl.semaphore_signal(barrier, inc=1, device_id=(other, d), device_id_type=MESH)
    for other in (right, left):
        pl.semaphore_signal(barrier, inc=1, device_id=(me, other), device_id_type=MESH)

    lanes = 128
    lane_row = lax.broadcasted_iota(jnp.int32, (lanes, TILE), 0)
    lane_col = lax.broadcasted_iota(jnp.int32, (lanes, TILE), 1)
    apart = jnp.where(
        lane_row < 3 * heads, lax.rem(lane_row, heads) - lax.div(lane_col, P_SIZE), -heads
    )
    for tile in range(width // TILE):
        e4[:, tile * TILE : (tile + 1) * TILE] = jnp.where(
            apart == tile * (TILE // P_SIZE), 1.0, 0.0
        ).astype(BF16)

    def pack(value):
        hi, mid, lo = split3(value)
        lane = lax.broadcasted_iota(jnp.int32, value.shape, 1)
        hi, mid, lo = hi.astype(F32), mid.astype(F32), lo.astype(F32)
        chosen = jnp.where(lane < heads, hi, jnp.where(lane < 2 * heads, mid, lo))
        return jnp.where(lane < 3 * heads, chosen, 0.0).astype(BF16)

    rep = jnp.where(
        lax.rem(lax.broadcasted_iota(jnp.int32, (heads, lanes), 1), heads)
        == lax.broadcasted_iota(jnp.int32, (heads, lanes), 0),
        1.0,
        0.0,
    ).astype(BF16)
    mask = lax.broadcasted_iota(jnp.int32, (Q, Q), 0) >= lax.broadcasted_iota(jnp.int32, (Q, Q), 1)
    low = jnp.where(mask, 1.0, 0.0).astype(BF16)

    def turned(parts, right_mat):
        total = 0.0
        for one in parts:
            total = total + lax.dot_general(
                one, right_mat, (((0,), (0,)), ((), ())), preferred_element_type=F32
            )
        return total

    def gap(b):
        return slice(b % 2 * Q, (b % 2 + 1) * Q), slice(b // 2 * lanes, (b // 2 + 1) * lanes)

    fades = slice(blocks // 2 * lanes, blocks // 2 * lanes + part)
    kept = slice(width - gw, width)

    mids, tots = [], []
    for b in range(blocks):
        rows = slice(b * Q, (b + 1) * Q)
        ld4 = turned(split3(ld_ref[:, rows]), rep)
        step4 = turned(split3(step_ref[:, rows]), rep)
        parts = split3(ld4)
        cum = dot(low, parts[0]) + dot(low, parts[1]) + dot(low, parts[2])
        mid = cum[Q // 2 - 1 : Q // 2, :]
        gbuf[gap(b)] = cum - mid
        u4[rows, :] = pack(step4 * jnp.exp(mid - cum))
        mids.append(mid)
        tots.append(cum[Q - 1 : Q, :])
    row = lax.broadcasted_iota(jnp.int32, (blocks, lanes), 0)
    zero = jnp.zeros((blocks, lanes), F32)
    m8, t8, o8, s8 = zero, zero, zero, zero
    run = jnp.zeros((1, lanes), F32)
    for b in range(blocks):
        m8 = jnp.where(row == b, mids[b], m8)
        t8 = jnp.where(row == b, tots[b], t8)
        o8 = jnp.where(row == b, run, o8)
        run = run + tots[b]
    dl_pair[0] = jnp.broadcast_to(run, (8, lanes))
    later = jnp.zeros((1, lanes), F32)
    for b in reversed(range(blocks)):
        s8 = jnp.where(row == b, later, s8)
        later = later + tots[b]
    rt[...] = dot(pack(jnp.exp(s8 + t8 - m8)), e4[...])
    fac[...] = jnp.zeros((N, width), F32)
    taps_x[...] = 0.5 * cwx[...]
    for k in range(KCONV):
        for g in range(groups):
            taps_bc[k : k + 1, g * 2 * N : (g + 1) * 2 * N] = 0.5 * cwbc[k, g : g + 1, :]

    def halo(q):
        src = bc_hbm.at[pl.ds(length - LEAD, LEAD)]
        dst = bcr.at[pl.ds(0, LEAD)]
        if q < strips:
            src = x_hbm.at[pl.ds(length - LEAD, LEAD), pl.ds(q * piece, piece)]
            dst = rs_send.at[pl.ds(q * strip, LEAD)]
        return pltpu.make_async_remote_copy(
            src_ref=src,
            dst_ref=dst,
            send_sem=halo_send.at[q],
            recv_sem=halo_recv.at[q],
            device_id=(after, d),
            device_id_type=MESH,
        )

    def to_seq(src, dst, send, recv, slot, there, other):
        return pltpu.make_async_remote_copy(
            src_ref=src.at[slot],
            dst_ref=dst.at[there],
            send_sem=send.at[0],
            recv_sem=recv.at[0],
            device_id=(other, d),
            device_id_type=MESH,
        )

    def all_of(ref, sem):
        others = ref.at[pl.ds(0, chips - 1)]
        return pltpu.make_async_copy(others, others, sem.at[0])

    def to_sibling(src, dst, slot):
        return pltpu.make_async_remote_copy(
            src_ref=src,
            dst_ref=dst,
            send_sem=pair_s.at[slot],
            recv_sem=pair_r.at[slot],
            device_id=(sibling, d),
            device_id_type=MESH,
        )

    def decays():
        return to_sibling(dl_pair.at[0], dl_pair.at[1], 2)

    def states(slot):
        return to_sibling(pair_send.at[slot], pair_recv.at[slot], slot)

    def conv(buf, taps, r0, cols, tap_cols):
        prev = buf[pl.ds(r0, LEAD), cols].astype(F32)[LEAD - 8 :]
        cur = buf[pl.ds(r0 + LEAD, Q), cols].astype(F32)
        ext = jnp.concatenate([prev, cur], 0)
        total = taps[KCONV - 1 : KCONV, tap_cols] * cur
        for k in range(1, KCONV):
            total = total + taps[KCONV - 1 - k : KCONV - k, tap_cols] * pltpu.roll(ext, k, 0)[8:]
        return total * jnp.tanh(total) + total

    def of_group(g, tile):
        return pl.ds(pl.multiple_of(g * gw + tile * TILE, TILE), TILE)

    def convolve(g, b):
        r0 = pl.multiple_of(b * Q, Q)
        both = pl.ds(pl.multiple_of(g * 2 * N, 2 * N), 2 * N)
        bcb[pl.ds(r0, Q), both] = conv(bcr, taps_bc, r0, both, both).astype(BF16)
        for k in range(gw // CONV_COLS):
            cols = pl.ds(pl.multiple_of(g * gw + k * CONV_COLS, CONV_COLS), CONV_COLS)
            inside = slice(k * CONV_COLS % piece, k * CONV_COLS % piece + CONV_COLS)
            q = g * per_group + k * CONV_COLS // piece
            xc = conv(rs_send, taps_x, pl.multiple_of(r0 + q * strip, LEAD), inside, cols).astype(BF16)
            xb[pl.ds(r0, Q), cols] = xc
            ub[pl.ds(r0, Q), cols] = (
                xc.astype(F32) * dot(u4[pl.ds(r0, Q), :], e4[:, cols])
            ).astype(BF16)

    def gather(g, b):
        r0 = pl.multiple_of(b * Q, Q)
        b_turned = bcb[pl.ds(r0, Q), pl.ds(pl.multiple_of(g * 2 * N, 2 * N), N)].astype(F32).T.astype(BF16)
        for tile in range(gw // TILE):
            cols = of_group(g, tile)
            fresh = dot(b_turned, ub[pl.ds(r0, Q), cols])
            pst[b, :, cols] = fresh
            fac[:, cols] = fac[:, cols] + rt[pl.ds(b, 1), cols] * fresh

    load_bc.wait()
    for q in range(strips):
        load_x(q).wait()
    load_z.start()
    load_w(0).start()
    load_w(1).start()

    def place(turn):
        early = turn < 2 * (blocks - 1)
        sent = (turn < blocks - 1) | (turn == 2 * (blocks - 1))
        return (
            jnp.where(sent, 1 - core, core),
            jnp.where(early, blocks - 1 - lax.rem(turn, blocks - 1), 0),
        )

    def first_pass(turn, carry):
        @pl.when(turn == blocks - 1)
        def _():
            pl.semaphore_wait(barrier, chips + 3)
            for q in range(strips + 1):
                halo(q).start()
            decays().start()

        @pl.when(turn == 2 * (blocks - 1))
        def _():
            for q in range(strips + 1):
                halo(q).wait_recv()

            @pl.when(me == 0)
            def _():
                for q in range(strips):
                    rs_send[q * strip : q * strip + LEAD, :] = jnp.zeros((LEAD, piece), BF16)
                bcr[:LEAD, :] = jnp.zeros((LEAD, bcr.shape[1]), BF16)

        gather(*place(turn - 1))
        convolve(*place(turn))

        @pl.when(turn == 2 * blocks - 1)
        def _():
            for tile in range(gw // TILE):
                pair_send[0, :, tile * TILE : (tile + 1) * TILE] = fac[
                    :, of_group(1 - core, tile)
                ].astype(BF16)
            states(0).start()

        return carry

    convolve(1 - core, blocks - 1)
    lax.fori_loop(1, 2 * blocks, first_pass, 0)
    gather(core, 0)

    decays().wait_recv()
    log_mine, log_other = dl_pair[0], dl_pair[1]
    first_core = core == 0
    of_core = pl.ds(pl.multiple_of(core * gw, gw), gw)
    fade_0 = dot(pack(jnp.exp(jnp.where(first_core, log_mine, log_other))), e4[:, of_core])
    fade_1 = dot(pack(jnp.exp(jnp.where(first_core, log_other, log_mine))), e4[:, of_core])
    fade_chip = pack(jnp.exp(log_mine + log_other)).astype(F32)
    fade_chip = jnp.concatenate([fade_chip, fade_chip], 0).astype(BF16)
    states(0).wait_recv()
    for rp in range(row_parts):
        for cp in range(col_parts):
            rows, cols = slice(rp * 16, (rp + 1) * 16), slice(cp * part, (cp + 1) * part)
            mine = fac[rows, pl.ds(pl.multiple_of(core * gw + cp * part, part), part)]
            other = pair_recv[0, rows, cols].astype(F32)
            state_0 = jnp.where(first_core, mine, other)
            state_1 = jnp.where(first_core, other, mine)
            faded = jnp.concatenate([fade_1[:, cols]] * 2, 0) * state_0
            gbuf[rows, width - gw + cp * part : width - gw + (cp + 1) * part] = state_0
            fmsg[rp * col_parts + cp, :, 0:part] = (faded + state_1).astype(BF16)
            fmsg[rp * col_parts + cp, :, part : part + lanes] = fade_chip

    def send_state(k, carry):
        j = lax.rem(chip + k, chips)
        to_seq(fmsg, frecv, f_s, f_r, j, chip, 2 * j + core).start()
        return carry

    lax.fori_loop(1, chips, send_state, 0)

    gbuf[N : N + 8, kept] = fade_0
    for ref, value in ((em, jnp.exp(m8)), (et, jnp.exp(t8 - m8)), (eo, jnp.exp(o8))):
        ref[...] = dot(pack(value), e4[...])
    parts = split3(jnp.broadcast_to(skip_ref[...], (8, heads)))
    skx[...] = dot(pack(dot(parts[0], rep) + dot(parts[1], rep) + dot(parts[2], rep)), e4[...])
    frecv_mine = fmsg[chip]
    for b in range(blocks):
        rows = slice(b * Q, (b + 1) * Q)
        a4[rows, :] = pack(jnp.exp(gbuf[gap(b)]))

    def recur(tile, carry):
        cols = pl.ds(pl.multiple_of(tile * 128, 128), 128)
        state = jnp.zeros((N, 128), F32)
        for b in range(blocks):
            fresh = pst[b, :, cols]
            pst[b, :, cols] = state
            state = et[b : b + 1, cols] * (fresh + em[b : b + 1, cols] * state)
        return carry

    lax.fori_loop(0, width // 128, recur, 0)

    all_of(frecv, f_r).wait()
    frecv[chip] = frecv_mine
    here = pl.multiple_of(core * gw + lax.rem(chip, col_parts) * part, part)
    arrived_fades = frecv[:, :, part : part + lanes].reshape(chips * 16, lanes)
    gbuf[: chips * 16, fades] = dot(arrived_fades, e4[:, pl.ds(here, part)])
    state = jnp.zeros((16, part), F32)
    for i in range(chips):
        imsg[i] = state.astype(BF16)
        state = gbuf[i * 16 : (i + 1) * 16, fades] * state + frecv[i, :, 0:part].astype(F32)

    def send_back(k, carry):
        j = lax.rem(chip + k, chips)
        to_seq(imsg, irecv, i_s, i_r, j, chip, 2 * j + core).start()
        return carry

    lax.fori_loop(1, chips, send_back, 0)
    irecv_mine = imsg[chip]
    all_of(irecv, i_r).wait()
    irecv[chip] = irecv_mine
    for rp in range(row_parts):
        for cp in range(col_parts):
            rows = slice(rp * 16, (rp + 1) * 16)
            cols = slice(width - gw + cp * part, width - gw + (cp + 1) * part)
            enters = irecv[rp * col_parts + cp].astype(F32)
            fade = gbuf[N : N + 8, cols]
            passed = jnp.concatenate([fade, fade], 0) * enters + gbuf[rows, cols]
            fac[rows, pl.ds(pl.multiple_of(core * gw + cp * part, part), part)] = jnp.where(
                first_core, enters, passed
            )
            pair_send[1, rows, cp * part : (cp + 1) * part] = jnp.where(
                first_core, passed, enters
            ).astype(BF16)
    states(1).start()
    load_z.wait()
    load_w(0).wait()
    load_w(1).wait()

    states(1).wait_recv()
    for tile in range(gw // TILE):
        fac[:, of_group(1 - core, tile)] = pair_recv[1, :, tile * TILE : (tile + 1) * TILE].astype(F32)

    def second_pass(chunk):
        for g in range(groups):
            for i in range(chunk_rows // Q):
                b = chunk * (chunk_rows // Q) + i
                r0 = pl.multiple_of(b * Q, Q)
                b_mat = bcb[pl.ds(r0, Q), slice(g * 2 * N, g * 2 * N + N)]
                c_mat = bcb[pl.ds(r0, Q), g * 2 * N + N : (g + 1) * 2 * N]
                scores = lax.dot_general(
                    c_mat, b_mat, (((1,), (1,)), ((), ())), preferred_element_type=F32
                )
                lhs = jnp.concatenate([jnp.where(mask, scores, 0.0).astype(BF16), c_mat], 1)
                for tile in range(gw // TILE):
                    cols = slice(g * gw + tile * TILE, g * gw + (tile + 1) * TILE)
                    entering = em[pl.ds(b, 1), cols] * (
                        pst[b, :, cols] + eo[pl.ds(b, 1), cols] * fac[:, cols]
                    )
                    rhs = jnp.concatenate([ub[pl.ds(r0, Q), cols], entering.astype(BF16)], 0)
                    y = dot(a4[pl.ds(r0, Q), :], e4[:, cols]) * dot(lhs, rhs)
                    y = y + skx[0:1, cols] * xb[pl.ds(r0, Q), cols].astype(F32)
                    z_half = 0.5 * zb[pl.ds(r0, Q), cols].astype(F32)
                    gbuf[i * Q : (i + 1) * Q, cols] = y * (z_half * jnp.tanh(z_half) + z_half)
        for i in range(chunk_rows // Q):
            r0 = pl.multiple_of((chunk * (chunk_rows // Q) + i) * Q, Q)
            for g in range(groups):
                squares = jnp.zeros((Q, 128), F32)
                for k in range(gw // 128):
                    gated = gbuf[i * Q : (i + 1) * Q, g * gw + k * 128 : g * gw + (k + 1) * 128]
                    squares = squares + gated * gated
                mean = jnp.sum(squares, axis=1, keepdims=True) * (1.0 / gw)
                scale = lax.rsqrt(mean + EPS)
                for tile in range(gw // TILE):
                    cols = slice(g * gw + tile * TILE, g * gw + (tile + 1) * TILE)
                    ub[pl.ds(r0, Q), cols] = (
                        gbuf[i * Q : (i + 1) * Q, cols] * scale * gain_ref[:, cols]
                    ).astype(BF16)

    def product(way, p, chunk):
        first = pl.multiple_of(way * half + p * piece, piece)
        rows = pl.ds(pl.multiple_of(chunk * chunk_rows, chunk_rows), chunk_rows)
        return dot(ub[rows, :], wb[:, pl.ds(first, piece)])

    def outgoing(way, turn, p):
        index = (lax.rem(turn, 2) * 2 + way) * PIECES + p
        return pl.ds(pl.multiple_of(index * chunk_rows, chunk_rows), chunk_rows)

    def hop(way, turn, p):
        return pltpu.make_async_remote_copy(
            src_ref=rs_send.at[outgoing(way, turn, p)],
            dst_ref=rs_recv.at[way, turn, p],
            send_sem=r_s.at[way, turn, p],
            recv_sem=r_r.at[way, turn, p],
            device_id=(me, jnp.where(way == 0, right, left)),
            device_id_type=MESH,
        )

    def stage(way, turn, p):
        chunk = lax.rem(jnp.where(way == 0, d + 2 * HEADS - 1 - turn, d + 1 + turn), HEADS)
        total = product(way, p, chunk)
        if not (isinstance(turn, int) and turn == 0):

            @pl.when(turn == 2)
            def _():
                hop(way, 0, p).wait_send()

            hop(way, turn - 1, p).wait_recv()
            total = total + rs_recv[way, turn - 1, p].astype(F32)
        rs_send[outgoing(way, turn, p), :] = total.astype(BF16)
        hop(way, turn, p).start()

    def first_stages(k, carry):
        @pl.when(k < 2)
        def _():
            second_pass(jnp.where(k == 0, left, right))

        stage(lax.rem(k, 2), 0, lax.div(k, 2))
        return carry

    lax.fori_loop(0, 2 * PIECES, first_stages, 0)

    def later_stages(k, carry):
        turn = 1 + lax.div(k, 2 * PIECES)
        q = lax.rem(k, 2 * PIECES)

        @pl.when(q == 0)
        def _():
            second_pass(lax.rem(jnp.where(turn == 1, d + 2, d), HEADS))

        stage(lax.rem(q, 2), turn, lax.div(q, 2))
        return carry

    lax.fori_loop(0, (HEADS - 2) * 2 * PIECES, later_stages, 0)

    def own(q, carry):
        total = product(lax.rem(q, 2), lax.div(q, 2), d)
        pst[q, :, 0:piece] = total[:Q]
        pst[q, :, piece : 2 * piece] = total[Q:]
        return carry

    lax.fori_loop(0, 2 * PIECES, own, 0)

    def to_out(way, p):
        first = pl.multiple_of(way * half + p * piece, piece)
        return pltpu.make_async_copy(
            zb.at[
                pl.ds(pl.multiple_of(way * chunk_rows, chunk_rows), chunk_rows),
                pl.ds(pl.multiple_of(p * piece, piece), piece),
            ],
            out_hbm.at[:, pl.ds(first, piece)],
            out_sem.at[way, p],
        )

    def finish(q, carry):
        way, p = lax.rem(q, 2), lax.div(q, 2)
        hop(way, HEADS - 2, p).wait_recv()
        arrived = rs_recv[way, HEADS - 2, p].astype(F32)
        cols = pl.ds(pl.multiple_of(p * piece, piece), piece)
        base = pl.multiple_of(way * chunk_rows, chunk_rows)
        zb[pl.ds(base, Q), cols] = (pst[q, :, 0:piece] + arrived[:Q]).astype(BF16)
        zb[pl.ds(base + Q, Q), cols] = (pst[q, :, piece : 2 * piece] + arrived[Q:]).astype(BF16)
        to_out(way, p).start()
        return carry

    lax.fori_loop(0, 2 * PIECES, finish, 0)

    for q in range(strips + 1):
        halo(q).wait_send()
    decays().wait_send()
    states(0).wait_send()
    states(1).wait_send()
    all_of(fmsg, f_s).wait()
    all_of(imsg, i_s).wait()

    def await_ring(q, carry):
        way, p = lax.rem(q, 2), lax.div(q, 2)
        for turn in range(1, HEADS - 1):
            hop(way, turn, p).wait_send()
        to_out(way, p).wait()
        return carry

    lax.fori_loop(0, 2 * PIECES, await_ring, 0)


def local(
    x_input,
    z_input,
    bc_input,
    conv_weight_x,
    conv_weight_bc,
    step_size,
    log_decay,
    skip_gain,
    norm_gain,
    out_weight,
):
    ns = lax.axis_size("seq")
    length, width = x_input.shape
    groups = bc_input.shape[1]
    columns = out_weight.shape[1]
    blocks = length // Q
    heads = step_size.shape[1]
    chips = ns // 2
    part = width // groups // (chips // (N // 16))
    piece = columns // 2 // PIECES
    rows = length // HEADS
    any_space = pl.BlockSpec(memory_space=pl.ANY)
    vmem = pl.BlockSpec(memory_space=pltpu.VMEM)
    dma = pltpu.SemaphoreType.DMA
    return pl.pallas_call(
        functools.partial(kernel, ns),
        out_shape=jax.ShapeDtypeStruct((rows, columns), BF16),
        in_specs=[any_space] * 4 + [vmem] * 6,
        out_specs=any_space,
        scratch_shapes=[
            pltpu.VMEM((length, width), BF16),
            pltpu.VMEM((length, width), BF16),
            pltpu.VMEM((LEAD + length, groups * 2 * N), BF16),
            pltpu.VMEM((length, groups * 2 * N), BF16),
            pltpu.VMEM((width, columns), BF16),
            pltpu.VMEM((length, width), BF16),
            pltpu.VMEM((blocks, N, width), F32),
            pltpu.VMEM((N, width), F32),
            pltpu.VMEM((128, width), BF16),
            pltpu.VMEM((length, 128), BF16),
            pltpu.VMEM((length, 128), BF16),
            pltpu.VMEM((blocks, width), F32),
            pltpu.VMEM((blocks, width), F32),
            pltpu.VMEM((blocks, width), F32),
            pltpu.VMEM((blocks, width), F32),
            pltpu.VMEM((8, width), F32),
            pltpu.VMEM((KCONV, width), F32),
            pltpu.VMEM((KCONV, groups * 2 * N), F32),
            pltpu.VMEM((2, 8, 128), F32),
            pltpu.VMEM((2, N, width // groups), BF16),
            pltpu.VMEM((2, N, width // groups), BF16),
            pltpu.VMEM((chips, 16, part + 128), BF16),
            pltpu.VMEM((chips, 16, part + 128), BF16),
            pltpu.VMEM((chips, 16, part), BF16),
            pltpu.VMEM((chips, 16, part), BF16),
            pltpu.VMEM((rows, width), F32),
            pltpu.VMEM((max(4 * PIECES * rows, width // piece * (LEAD + length)), piece), BF16),
            pltpu.VMEM((2, HEADS - 1, PIECES, rows, piece), BF16),
            dma((width // piece + 4,)),
            dma((width // piece + 1,)),
            dma((width // piece + 1,)),
            dma((3,)),
            dma((3,)),
            dma((1,)),
            dma((1,)),
            dma((1,)),
            dma((1,)),
            dma((2, HEADS - 1, PIECES)),
            dma((2, HEADS - 1, PIECES)),
            dma((2, PIECES)),
        ],
        compiler_params=pltpu.CompilerParams(
            collective_id=0, has_side_effects=True, vmem_limit_bytes=60 * 2**20
        ),
        cost_estimate=pl.CostEstimate(
            flops=2 * length * width * columns,
            bytes_accessed=2 * (2 * length * width + width * columns),
            transcendentals=2 * length * width,
        ),
    )(
        x_input,
        z_input,
        bc_input.reshape(length, groups * 2 * N),
        out_weight,
        conv_weight_x,
        conv_weight_bc,
        step_size.T,
        log_decay.T,
        skip_gain.reshape(1, heads),
        norm_gain.reshape(1, width),
    )


def solution(mesh):
    in_specs = (
        P("seq", "head"),
        P("seq", "head"),
        P("seq", "head", None),
        P(None, "head"),
        P(None, "head", None),
        P("seq", "head"),
        P("seq", "head"),
        P("head"),
        P("head"),
        P("head", None),
    )
    out_specs = P(("seq", "head"), None)
    return jax.shard_map(local, mesh=mesh, in_specs=in_specs, out_specs=out_specs, check_vma=False)
```

```python
import functools

import jax
import jax.numpy as jnp
from jax import lax
from jax.experimental import pallas as pl
from jax.experimental.pallas import tpu as pltpu
from jax.sharding import PartitionSpec as P

P_SIZE = 64
N = 128
KCONV = 4
EPS = 1e-05
Q = 128
LEAD = 16
TILE = 256
CONV_COLS = 256
PIECES = 4
HEADS = 4

MESH = pl.DeviceIdType.MESH
F32 = jnp.float32
BF16 = jnp.bfloat16


def split3(value):
    hi = value.astype(BF16)
    rest = value - hi.astype(F32)
    mid = rest.astype(BF16)
    return hi, mid, (rest - mid.astype(F32)).astype(BF16)


def dot(a, b):
    return jnp.dot(a, b, preferred_element_type=F32)


def kernel(
    ns,
    x_hbm,
    z_hbm,
    bc_hbm,
    w_hbm,
    cwx,
    cwbc,
    step_ref,
    ld_ref,
    skip_ref,
    gain_ref,
    out_hbm,
    xb,
    zb,
    bcr,
    bcb,
    wb,
    ub,
    pst,
    fac,
    e4,
    a4,
    u4,
    em,
    et,
    eo,
    rt,
    skx,
    taps_x,
    taps_bc,
    dl_pair,
    pair_send,
    pair_recv,
    fmsg,
    frecv,
    imsg,
    irecv,
    gbuf,
    rs_send,
    rs_recv,
    local_sem,
    halo_send,
    halo_recv,
    pair_s,
    pair_r,
    f_s,
    f_r,
    i_s,
    i_r,
    r_s,
    r_r,
    out_sem,
):
    length, width = x_hbm.shape
    columns = w_hbm.shape[1]
    heads = step_ref.shape[0]
    groups = bc_hbm.shape[1] // (2 * N)
    gw = width // groups
    blocks = length // Q
    chunk_rows = length // HEADS
    half = columns // 2
    piece = half // PIECES
    chips = ns // 2
    row_parts = N // 16
    col_parts = chips // row_parts
    part = gw // col_parts
    strip = LEAD + length
    strips = width // piece

    me = lax.axis_index("seq")
    d = lax.axis_index("head")
    right = lax.rem(d + 1, HEADS)
    left = lax.rem(d + HEADS - 1, HEADS)
    after = lax.rem(me + 1, ns)
    chip, core = lax.div(me, 2), lax.rem(me, 2)
    sibling = me + 1 - 2 * core

    barrier = pltpu.get_barrier_semaphore()

    def load_x(q):
        return pltpu.make_async_copy(
            x_hbm.at[:, pl.ds(pl.multiple_of(q * piece, piece), piece)],
            rs_send.at[pl.ds(pl.multiple_of(q * strip + LEAD, LEAD), length)],
            local_sem.at[q],
        )

    load_bc = pltpu.make_async_copy(bc_hbm, bcr.at[pl.ds(LEAD, length)], local_sem.at[strips])
    load_z = pltpu.make_async_copy(z_hbm, zb, local_sem.at[strips + 1])

    def load_w(h):
        return pltpu.make_async_copy(
            w_hbm.at[:, pl.ds(h * half, half)],
            wb.at[:, pl.ds(h * half, half)],
            local_sem.at[strips + 2 + h],
        )

    load_bc.start()
    per_group = strips // groups
    for q in range(per_group):
        load_x((1 - core) * per_group + q).start()
    for q in range(per_group):
        load_x(core * per_group + q).start()

    def greet(k, carry):
        other = 2 * lax.rem(chip + k, chips) + core
        pl.semaphore_signal(barrier, inc=1, device_id=(other, d), device_id_type=MESH)
        return carry

    lax.fori_loop(1, chips, greet, 0)
    across = lax.rem(jnp.where(core == 0, me + ns - 1, me + 1), ns)
    for other in (sibling, across):
        pl.semaphore_signal(barrier, inc=1, device_id=(other, d), device_id_type=MESH)
    for other in (right, left):
        pl.semaphore_signal(barrier, inc=1, device_id=(me, other), device_id_type=MESH)

    lanes = 128
    lane_row = lax.broadcasted_iota(jnp.int32, (lanes, TILE), 0)
    lane_col = lax.broadcasted_iota(jnp.int32, (lanes, TILE), 1)
    apart = jnp.where(
        lane_row < 3 * heads, lax.rem(lane_row, heads) - lax.div(lane_col, P_SIZE), -heads
    )
    for tile in range(width // TILE):
        e4[:, tile * TILE : (tile + 1) * TILE] = jnp.where(
            apart == tile * (TILE // P_SIZE), 1.0, 0.0
        ).astype(BF16)

    def pack(value):
        hi, mid, lo = split3(value)
        lane = lax.broadcasted_iota(jnp.int32, value.shape, 1)
        hi, mid, lo = hi.astype(F32), mid.astype(F32), lo.astype(F32)
        chosen = jnp.where(lane < heads, hi, jnp.where(lane < 2 * heads, mid, lo))
        return jnp.where(lane < 3 * heads, chosen, 0.0).astype(BF16)

    rep = jnp.where(
        lax.rem(lax.broadcasted_iota(jnp.int32, (heads, lanes), 1), heads)
        == lax.broadcasted_iota(jnp.int32, (heads, lanes), 0),
        1.0,
        0.0,
    ).astype(BF16)
    mask = lax.broadcasted_iota(jnp.int32, (Q, Q), 0) >= lax.broadcasted_iota(jnp.int32, (Q, Q), 1)
    low = jnp.where(mask, 1.0, 0.0).astype(BF16)

    def turned(parts, right_mat):
        total = 0.0
        for one in parts:
            total = total + lax.dot_general(
                one, right_mat, (((0,), (0,)), ((), ())), preferred_element_type=F32
            )
        return total

    def gap(b):
        return slice(b % 2 * Q, (b % 2 + 1) * Q), slice(b // 2 * lanes, (b // 2 + 1) * lanes)

    fades = slice(blocks // 2 * lanes, blocks // 2 * lanes + part)
    kept = slice(width - gw, width)

    mids, tots = [], []
    for b in range(blocks):
        rows = slice(b * Q, (b + 1) * Q)
        ld4 = turned(split3(ld_ref[:, rows]), rep)
        step4 = turned(split3(step_ref[:, rows]), rep)
        parts = split3(ld4)
        cum = dot(low, parts[0]) + dot(low, parts[1]) + dot(low, parts[2])
        mid = cum[Q // 2 - 1 : Q // 2, :]
        gbuf[gap(b)] = cum - mid
        u4[rows, :] = pack(step4 * jnp.exp(mid - cum))
        mids.append(mid)
        tots.append(cum[Q - 1 : Q, :])
    row = lax.broadcasted_iota(jnp.int32, (blocks, lanes), 0)
    zero = jnp.zeros((blocks, lanes), F32)
    m8, t8, o8, s8 = zero, zero, zero, zero
    run = jnp.zeros((1, lanes), F32)
    for b in range(blocks):
        m8 = jnp.where(row == b, mids[b], m8)
        t8 = jnp.where(row == b, tots[b], t8)
        o8 = jnp.where(row == b, run, o8)
        run = run + tots[b]
    dl_pair[0] = jnp.broadcast_to(run, (8, lanes))
    later = jnp.zeros((1, lanes), F32)
    for b in reversed(range(blocks)):
        s8 = jnp.where(row == b, later, s8)
        later = later + tots[b]
    rt[...] = dot(pack(jnp.exp(s8 + t8 - m8)), e4[...])
    fac[...] = jnp.zeros((N, width), F32)
    taps_x[...] = 0.5 * cwx[...]
    for k in range(KCONV):
        for g in range(groups):
            taps_bc[k : k + 1, g * 2 * N : (g + 1) * 2 * N] = 0.5 * cwbc[k, g : g + 1, :]

    def halo(q):
        src = bc_hbm.at[pl.ds(length - LEAD, LEAD)]
        dst = bcr.at[pl.ds(0, LEAD)]
        if q < strips:
            src = x_hbm.at[pl.ds(length - LEAD, LEAD), pl.ds(q * piece, piece)]
            dst = rs_send.at[pl.ds(q * strip, LEAD)]
        return pltpu.make_async_remote_copy(
            src_ref=src,
            dst_ref=dst,
            send_sem=halo_send.at[q],
            recv_sem=halo_recv.at[q],
            device_id=(after, d),
            device_id_type=MESH,
        )

    def to_seq(src, dst, send, recv, slot, there, other):
        return pltpu.make_async_remote_copy(
            src_ref=src.at[slot],
            dst_ref=dst.at[there],
            send_sem=send.at[0],
            recv_sem=recv.at[0],
            device_id=(other, d),
            device_id_type=MESH,
        )

    def all_of(ref, sem):
        others = ref.at[pl.ds(0, chips - 1)]
        return pltpu.make_async_copy(others, others, sem.at[0])

    def to_sibling(src, dst, slot):
        return pltpu.make_async_remote_copy(
            src_ref=src,
            dst_ref=dst,
            send_sem=pair_s.at[slot],
            recv_sem=pair_r.at[slot],
            device_id=(sibling, d),
            device_id_type=MESH,
        )

    def decays():
        return to_sibling(dl_pair.at[0], dl_pair.at[1], 2)

    def states(slot):
        return to_sibling(pair_send.at[slot], pair_recv.at[slot], slot)

    def conv(buf, taps, r0, cols, tap_cols):
        prev = buf[pl.ds(r0, LEAD), cols].astype(F32)[LEAD - 8 :]
        cur = buf[pl.ds(r0 + LEAD, Q), cols].astype(F32)
        ext = jnp.concatenate([prev, cur], 0)
        total = taps[KCONV - 1 : KCONV, tap_cols] * cur
        for k in range(1, KCONV):
            total = total + taps[KCONV - 1 - k : KCONV - k, tap_cols] * pltpu.roll(ext, k, 0)[8:]
        return total * jnp.tanh(total) + total

    def of_group(g, tile):
        return pl.ds(pl.multiple_of(g * gw + tile * TILE, TILE), TILE)

    def convolve(g, b):
        r0 = pl.multiple_of(b * Q, Q)
        both = pl.ds(pl.multiple_of(g * 2 * N, 2 * N), 2 * N)
        bcb[pl.ds(r0, Q), both] = conv(bcr, taps_bc, r0, both, both).astype(BF16)
        for k in range(gw // CONV_COLS):
            cols = pl.ds(pl.multiple_of(g * gw + k * CONV_COLS, CONV_COLS), CONV_COLS)
            inside = slice(k * CONV_COLS % piece, k * CONV_COLS % piece + CONV_COLS)
            q = g * per_group + k * CONV_COLS // piece
            xc = conv(rs_send, taps_x, pl.multiple_of(r0 + q * strip, LEAD), inside, cols).astype(BF16)
            xb[pl.ds(r0, Q), cols] = xc
            ub[pl.ds(r0, Q), cols] = (
                xc.astype(F32) * dot(u4[pl.ds(r0, Q), :], e4[:, cols])
            ).astype(BF16)

    def gather(g, b):
        r0 = pl.multiple_of(b * Q, Q)
        b_turned = bcb[pl.ds(r0, Q), pl.ds(pl.multiple_of(g * 2 * N, 2 * N), N)].astype(F32).T.astype(BF16)
        for tile in range(gw // TILE):
            cols = of_group(g, tile)
            fresh = dot(b_turned, ub[pl.ds(r0, Q), cols])
            pst[b, :, cols] = fresh
            fac[:, cols] = fac[:, cols] + rt[pl.ds(b, 1), cols] * fresh

    load_bc.wait()
    for q in range(per_group):
        load_x((1 - core) * per_group + q).wait()

    lead_turn = blocks + blocks // 2 - 1

    def place(turn):
        sent = (turn < blocks - 1) | (turn == lead_turn)
        others = jnp.where(turn < lead_turn, 2 * blocks - 2 - turn, 2 * blocks - 1 - turn)
        return (
            jnp.where(sent, 1 - core, core),
            jnp.where(turn < blocks - 1, blocks - 1 - turn, jnp.where(turn == lead_turn, 0, others)),
        )

    def first_pass(turn, carry):
        @pl.when(turn == blocks - 1)
        def _():
            for q in range(per_group):
                load_x(core * per_group + q).wait()
            load_z.start()
            load_w(0).start()
            load_w(1).start()

        @pl.when(turn == blocks - 3)
        def _():
            pl.semaphore_wait(barrier, chips + 3)
            for q in range(strips + 1):
                halo(q).start()
            decays().start()

        @pl.when(turn == lead_turn)
        def _():
            for q in range(strips + 1):
                halo(q).wait_recv()

            @pl.when(me == 0)
            def _():
                for q in range(strips):
                    rs_send[q * strip : q * strip + LEAD, :] = jnp.zeros((LEAD, piece), BF16)
                bcr[:LEAD, :] = jnp.zeros((LEAD, bcr.shape[1]), BF16)

        gather(*place(turn - 1))
        convolve(*place(turn))

        @pl.when(turn == lead_turn + 1)
        def _():
            for tile in range(gw // TILE):
                pair_send[0, :, tile * TILE : (tile + 1) * TILE] = fac[
                    :, of_group(1 - core, tile)
                ].astype(BF16)
            states(0).start()

        return carry

    convolve(1 - core, blocks - 1)
    lax.fori_loop(1, 2 * blocks, first_pass, 0)
    gather(core, 0)

    decays().wait_recv()
    log_mine, log_other = dl_pair[0], dl_pair[1]
    first_core = core == 0
    of_core = pl.ds(pl.multiple_of(core * gw, gw), gw)
    fade_0 = dot(pack(jnp.exp(jnp.where(first_core, log_mine, log_other))), e4[:, of_core])
    fade_1 = dot(pack(jnp.exp(jnp.where(first_core, log_other, log_mine))), e4[:, of_core])
    fade_chip = pack(jnp.exp(log_mine + log_other)).astype(F32)
    fade_chip = jnp.concatenate([fade_chip, fade_chip], 0).astype(BF16)
    states(0).wait_recv()
    for rp in range(row_parts):
        for cp in range(col_parts):
            rows, cols = slice(rp * 16, (rp + 1) * 16), slice(cp * part, (cp + 1) * part)
            mine = fac[rows, pl.ds(pl.multiple_of(core * gw + cp * part, part), part)]
            other = pair_recv[0, rows, cols].astype(F32)
            state_0 = jnp.where(first_core, mine, other)
            state_1 = jnp.where(first_core, other, mine)
            faded = jnp.concatenate([fade_1[:, cols]] * 2, 0) * state_0
            gbuf[rows, width - gw + cp * part : width - gw + (cp + 1) * part] = state_0
            fmsg[rp * col_parts + cp, :, 0:part] = (faded + state_1).astype(BF16)
            fmsg[rp * col_parts + cp, :, part : part + lanes] = fade_chip

    def send_state(k, carry):
        j = lax.rem(chip + k, chips)
        to_seq(fmsg, frecv, f_s, f_r, j, chip, 2 * j + core).start()
        return carry

    lax.fori_loop(1, chips, send_state, 0, unroll=True)

    gbuf[N : N + 8, kept] = fade_0
    for ref, value in ((em, jnp.exp(m8)), (et, jnp.exp(t8 - m8)), (eo, jnp.exp(o8))):
        ref[...] = dot(pack(value), e4[...])
    parts = split3(jnp.broadcast_to(skip_ref[...], (8, heads)))
    skx[...] = dot(pack(dot(parts[0], rep) + dot(parts[1], rep) + dot(parts[2], rep)), e4[...])
    frecv_mine = fmsg[chip]
    for b in range(blocks):
        rows = slice(b * Q, (b + 1) * Q)
        a4[rows, :] = pack(jnp.exp(gbuf[gap(b)]))

    def recur(tile, carry):
        cols = pl.ds(pl.multiple_of(tile * 128, 128), 128)
        state = jnp.zeros((N, 128), F32)
        for b in range(blocks):
            fresh = pst[b, :, cols]
            pst[b, :, cols] = state
            state = et[b : b + 1, cols] * (fresh + em[b : b + 1, cols] * state)
        return carry

    lax.fori_loop(0, width // 128, recur, 0)

    all_of(frecv, f_r).wait()
    frecv[chip] = frecv_mine
    here = pl.multiple_of(core * gw + lax.rem(chip, col_parts) * part, part)
    arrived_fades = frecv[:, :, part : part + lanes].reshape(chips * 16, lanes)
    gbuf[: chips * 16, fades] = dot(arrived_fades, e4[:, pl.ds(here, part)])
    state = jnp.zeros((16, part), F32)
    for i in range(chips):
        imsg[i] = state.astype(BF16)
        state = gbuf[i * 16 : (i + 1) * 16, fades] * state + frecv[i, :, 0:part].astype(F32)

    def send_back(k, carry):
        j = lax.rem(chip + k, chips)
        to_seq(imsg, irecv, i_s, i_r, j, chip, 2 * j + core).start()
        return carry

    lax.fori_loop(1, chips, send_back, 0, unroll=True)
    irecv_mine = imsg[chip]
    all_of(irecv, i_r).wait()
    irecv[chip] = irecv_mine
    for rp in range(row_parts):
        for cp in range(col_parts):
            rows = slice(rp * 16, (rp + 1) * 16)
            cols = slice(width - gw + cp * part, width - gw + (cp + 1) * part)
            enters = irecv[rp * col_parts + cp].astype(F32)
            fade = gbuf[N : N + 8, cols]
            passed = jnp.concatenate([fade, fade], 0) * enters + gbuf[rows, cols]
            fac[rows, pl.ds(pl.multiple_of(core * gw + cp * part, part), part)] = jnp.where(
                first_core, enters, passed
            )
            pair_send[1, rows, cp * part : (cp + 1) * part] = jnp.where(
                first_core, passed, enters
            ).astype(BF16)
    states(1).start()
    load_z.wait()
    load_w(0).wait()
    load_w(1).wait()

    states(1).wait_recv()
    for tile in range(gw // TILE):
        fac[:, of_group(1 - core, tile)] = pair_recv[1, :, tile * TILE : (tile + 1) * TILE].astype(F32)

    def second_pass(chunk):
        for g in range(groups):
            for i in range(chunk_rows // Q):
                b = chunk * (chunk_rows // Q) + i
                r0 = pl.multiple_of(b * Q, Q)
                b_mat = bcb[pl.ds(r0, Q), slice(g * 2 * N, g * 2 * N + N)]
                c_mat = bcb[pl.ds(r0, Q), g * 2 * N + N : (g + 1) * 2 * N]
                scores = lax.dot_general(
                    c_mat, b_mat, (((1,), (1,)), ((), ())), preferred_element_type=F32
                )
                lhs = jnp.concatenate([jnp.where(mask, scores, 0.0).astype(BF16), c_mat], 1)
                for tile in range(gw // TILE):
                    cols = slice(g * gw + tile * TILE, g * gw + (tile + 1) * TILE)
                    entering = em[pl.ds(b, 1), cols] * (
                        pst[b, :, cols] + eo[pl.ds(b, 1), cols] * fac[:, cols]
                    )
                    rhs = jnp.concatenate([ub[pl.ds(r0, Q), cols], entering.astype(BF16)], 0)
                    y = dot(a4[pl.ds(r0, Q), :], e4[:, cols]) * dot(lhs, rhs)
                    y = y + skx[0:1, cols] * xb[pl.ds(r0, Q), cols].astype(F32)
                    z_half = 0.5 * zb[pl.ds(r0, Q), cols].astype(F32)
                    gbuf[i * Q : (i + 1) * Q, cols] = y * (z_half * jnp.tanh(z_half) + z_half)
        for i in range(chunk_rows // Q):
            r0 = pl.multiple_of((chunk * (chunk_rows // Q) + i) * Q, Q)
            for g in range(groups):
                squares = jnp.zeros((Q, 128), F32)
                for k in range(gw // 128):
                    gated = gbuf[i * Q : (i + 1) * Q, g * gw + k * 128 : g * gw + (k + 1) * 128]
                    squares = squares + gated * gated
                mean = jnp.sum(squares, axis=1, keepdims=True) * (1.0 / gw)
                scale = lax.rsqrt(mean + EPS)
                for tile in range(gw // TILE):
                    cols = slice(g * gw + tile * TILE, g * gw + (tile + 1) * TILE)
                    ub[pl.ds(r0, Q), cols] = (
                        gbuf[i * Q : (i + 1) * Q, cols] * scale * gain_ref[:, cols]
                    ).astype(BF16)

    def product(way, p, chunk):
        first = pl.multiple_of(way * half + p * piece, piece)
        rows = pl.ds(pl.multiple_of(chunk * chunk_rows, chunk_rows), chunk_rows)
        return dot(ub[rows, :], wb[:, pl.ds(first, piece)])

    def outgoing(way, turn, p):
        index = (lax.rem(turn, 2) * 2 + way) * PIECES + p
        return pl.ds(pl.multiple_of(index * chunk_rows, chunk_rows), chunk_rows)

    def hop(way, turn, p):
        return pltpu.make_async_remote_copy(
            src_ref=rs_send.at[outgoing(way, turn, p)],
            dst_ref=rs_recv.at[way, turn, p],
            send_sem=r_s.at[way, turn, p],
            recv_sem=r_r.at[way, turn, p],
            device_id=(me, jnp.where(way == 0, right, left)),
            device_id_type=MESH,
        )

    def stage(way, turn, p):
        chunk = lax.rem(jnp.where(way == 0, d + 2 * HEADS - 1 - turn, d + 1 + turn), HEADS)
        total = product(way, p, chunk)
        if not (isinstance(turn, int) and turn == 0):

            @pl.when(turn == 2)
            def _():
                hop(way, 0, p).wait_send()

            hop(way, turn - 1, p).wait_recv()
            total = total + rs_recv[way, turn - 1, p].astype(F32)
        rs_send[outgoing(way, turn, p), :] = total.astype(BF16)
        hop(way, turn, p).start()

    def first_stages(k, carry):
        @pl.when(k < 2)
        def _():
            second_pass(jnp.where(k == 0, left, right))

        stage(lax.rem(k, 2), 0, lax.div(k, 2))
        return carry

    lax.fori_loop(0, 2 * PIECES, first_stages, 0)

    def later_stages(k, carry):
        turn = 1 + lax.div(k, 2 * PIECES)
        q = lax.rem(k, 2 * PIECES)

        @pl.when(q == 0)
        def _():
            second_pass(lax.rem(jnp.where(turn == 1, d + 2, d), HEADS))

        stage(lax.rem(q, 2), turn, lax.div(q, 2))
        return carry

    lax.fori_loop(0, (HEADS - 2) * 2 * PIECES, later_stages, 0)

    def own(q, carry):
        total = product(lax.rem(q, 2), lax.div(q, 2), d)
        pst[q, :, 0:piece] = total[:Q]
        pst[q, :, piece : 2 * piece] = total[Q:]
        return carry

    lax.fori_loop(0, 2 * PIECES, own, 0)

    def to_out(way, p):
        first = pl.multiple_of(way * half + p * piece, piece)
        return pltpu.make_async_copy(
            zb.at[
                pl.ds(pl.multiple_of(way * chunk_rows, chunk_rows), chunk_rows),
                pl.ds(pl.multiple_of(p * piece, piece), piece),
            ],
            out_hbm.at[:, pl.ds(first, piece)],
            out_sem.at[way, p],
        )

    def finish(q, carry):
        way, p = lax.rem(q, 2), lax.div(q, 2)
        hop(way, HEADS - 2, p).wait_recv()
        arrived = rs_recv[way, HEADS - 2, p].astype(F32)
        cols = pl.ds(pl.multiple_of(p * piece, piece), piece)
        base = pl.multiple_of(way * chunk_rows, chunk_rows)
        zb[pl.ds(base, Q), cols] = (pst[q, :, 0:piece] + arrived[:Q]).astype(BF16)
        zb[pl.ds(base + Q, Q), cols] = (pst[q, :, piece : 2 * piece] + arrived[Q:]).astype(BF16)
        to_out(way, p).start()
        return carry

    lax.fori_loop(0, 2 * PIECES, finish, 0)

    for q in range(strips + 1):
        halo(q).wait_send()
    decays().wait_send()
    states(0).wait_send()
    states(1).wait_send()
    all_of(fmsg, f_s).wait()
    all_of(imsg, i_s).wait()

    def await_ring(q, carry):
        way, p = lax.rem(q, 2), lax.div(q, 2)
        for turn in range(1, HEADS - 1):
            hop(way, turn, p).wait_send()
        to_out(way, p).wait()
        return carry

    lax.fori_loop(0, 2 * PIECES, await_ring, 0)


def local(
    x_input,
    z_input,
    bc_input,
    conv_weight_x,
    conv_weight_bc,
    step_size,
    log_decay,
    skip_gain,
    norm_gain,
    out_weight,
):
    ns = lax.axis_size("seq")
    length, width = x_input.shape
    groups = bc_input.shape[1]
    columns = out_weight.shape[1]
    blocks = length // Q
    heads = step_size.shape[1]
    chips = ns // 2
    part = width // groups // (chips // (N // 16))
    piece = columns // 2 // PIECES
    rows = length // HEADS
    any_space = pl.BlockSpec(memory_space=pl.ANY)
    vmem = pl.BlockSpec(memory_space=pltpu.VMEM)
    dma = pltpu.SemaphoreType.DMA
    return pl.pallas_call(
        functools.partial(kernel, ns),
        out_shape=jax.ShapeDtypeStruct((rows, columns), BF16),
        in_specs=[any_space] * 4 + [vmem] * 6,
        out_specs=any_space,
        scratch_shapes=[
            pltpu.VMEM((length, width), BF16),
            pltpu.VMEM((length, width), BF16),
            pltpu.VMEM((LEAD + length, groups * 2 * N), BF16),
            pltpu.VMEM((length, groups * 2 * N), BF16),
            pltpu.VMEM((width, columns), BF16),
            pltpu.VMEM((length, width), BF16),
            pltpu.VMEM((blocks, N, width), F32),
            pltpu.VMEM((N, width), F32),
            pltpu.VMEM((128, width), BF16),
            pltpu.VMEM((length, 128), BF16),
            pltpu.VMEM((length, 128), BF16),
            pltpu.VMEM((blocks, width), F32),
            pltpu.VMEM((blocks, width), F32),
            pltpu.VMEM((blocks, width), F32),
            pltpu.VMEM((blocks, width), F32),
            pltpu.VMEM((8, width), F32),
            pltpu.VMEM((KCONV, width), F32),
            pltpu.VMEM((KCONV, groups * 2 * N), F32),
            pltpu.VMEM((2, 8, 128), F32),
            pltpu.VMEM((2, N, width // groups), BF16),
            pltpu.VMEM((2, N, width // groups), BF16),
            pltpu.VMEM((chips, 16, part + 128), BF16),
            pltpu.VMEM((chips, 16, part + 128), BF16),
            pltpu.VMEM((chips, 16, part), BF16),
            pltpu.VMEM((chips, 16, part), BF16),
            pltpu.VMEM((rows, width), F32),
            pltpu.VMEM((max(4 * PIECES * rows, width // piece * (LEAD + length)), piece), BF16),
            pltpu.VMEM((2, HEADS - 1, PIECES, rows, piece), BF16),
            dma((width // piece + 4,)),
            dma((width // piece + 1,)),
            dma((width // piece + 1,)),
            dma((3,)),
            dma((3,)),
            dma((1,)),
            dma((1,)),
            dma((1,)),
            dma((1,)),
            dma((2, HEADS - 1, PIECES)),
            dma((2, HEADS - 1, PIECES)),
            dma((2, PIECES)),
        ],
        compiler_params=pltpu.CompilerParams(
            collective_id=0, has_side_effects=True, vmem_limit_bytes=60 * 2**20
        ),
        cost_estimate=pl.CostEstimate(
            flops=2 * length * width * columns,
            bytes_accessed=2 * (2 * length * width + width * columns),
            transcendentals=2 * length * width,
        ),
    )(
        x_input,
        z_input,
        bc_input.reshape(length, groups * 2 * N),
        out_weight,
        conv_weight_x,
        conv_weight_bc,
        step_size.T,
        log_decay.T,
        skip_gain.reshape(1, heads),
        norm_gain.reshape(1, width),
    )


def solution(mesh):
    in_specs = (
        P("seq", "head"),
        P("seq", "head"),
        P("seq", "head", None),
        P(None, "head"),
        P(None, "head", None),
        P("seq", "head"),
        P("seq", "head"),
        P("head"),
        P("head"),
        P("head", None),
    )
    out_specs = P(("seq", "head"), None)
    return jax.shard_map(local, mesh=mesh, in_specs=in_specs, out_specs=out_specs, check_vma=False)
```

```python
import functools

import jax
import jax.numpy as jnp
from jax import lax
from jax.experimental import pallas as pl
from jax.experimental.pallas import tpu as pltpu
from jax.sharding import PartitionSpec as P

P_SIZE = 64
N = 128
KCONV = 4
EPS = 1e-05
Q = 128
LEAD = 16
TILE = 256
CONV_COLS = 256
PIECES = 4
HEADS = 4

MESH = pl.DeviceIdType.MESH
F32 = jnp.float32
BF16 = jnp.bfloat16


def split3(value):
    hi = value.astype(BF16)
    rest = value - hi.astype(F32)
    mid = rest.astype(BF16)
    return hi, mid, (rest - mid.astype(F32)).astype(BF16)


def dot(a, b):
    return jnp.dot(a, b, preferred_element_type=F32)


def kernel(
    ns,
    x_hbm,
    z_hbm,
    bc_hbm,
    w_hbm,
    cwx,
    cwbc,
    step_ref,
    ld_ref,
    skip_ref,
    gain_ref,
    out_hbm,
    xb,
    zb,
    bcr,
    bcb,
    wb,
    ub,
    pst,
    fac,
    e4,
    a4,
    u4,
    em,
    et,
    eo,
    rt,
    skx,
    taps_x,
    taps_bc,
    dl_pair,
    pair_send,
    pair_recv,
    fmsg,
    frecv,
    imsg,
    irecv,
    gbuf,
    rs_send,
    rs_recv,
    local_sem,
    halo_send,
    halo_recv,
    pair_s,
    pair_r,
    f_s,
    f_r,
    i_s,
    i_r,
    r_s,
    r_r,
    out_sem,
):
    length, width = x_hbm.shape
    columns = w_hbm.shape[1]
    heads = step_ref.shape[0]
    groups = bc_hbm.shape[1] // (2 * N)
    gw = width // groups
    blocks = length // Q
    chunk_rows = length // HEADS
    half = columns // 2
    piece = half // PIECES
    chips = ns // 2
    row_parts = N // 16
    col_parts = chips // row_parts
    part = gw // col_parts
    strip = LEAD + length
    strips = width // piece

    me = lax.axis_index("seq")
    d = lax.axis_index("head")
    right = lax.rem(d + 1, HEADS)
    left = lax.rem(d + HEADS - 1, HEADS)
    after = lax.rem(me + 1, ns)
    chip, core = lax.div(me, 2), lax.rem(me, 2)
    sibling = me + 1 - 2 * core

    barrier = pltpu.get_barrier_semaphore()

    def load_x(q):
        return pltpu.make_async_copy(
            x_hbm.at[:, pl.ds(pl.multiple_of(q * piece, piece), piece)],
            rs_send.at[pl.ds(pl.multiple_of(q * strip + LEAD, LEAD), length)],
            local_sem.at[q],
        )

    load_bc = pltpu.make_async_copy(bc_hbm, bcr.at[pl.ds(LEAD, length)], local_sem.at[strips])
    load_z = pltpu.make_async_copy(z_hbm, zb, local_sem.at[strips + 1])

    def load_w(h):
        return pltpu.make_async_copy(
            w_hbm.at[:, pl.ds(h * half, half)],
            wb.at[:, pl.ds(h * half, half)],
            local_sem.at[strips + 2 + h],
        )

    load_bc.start()
    per_group = strips // groups
    for q in range(per_group):
        load_x((1 - core) * per_group + q).start()
    for q in range(per_group):
        load_x(core * per_group + q).start()

    def greet(k, carry):
        other = 2 * lax.rem(chip + k, chips) + core
        pl.semaphore_signal(barrier, inc=1, device_id=(other, d), device_id_type=MESH)
        return carry

    lax.fori_loop(1, chips, greet, 0)
    across = lax.rem(jnp.where(core == 0, me + ns - 1, me + 1), ns)
    for other in (sibling, across):
        pl.semaphore_signal(barrier, inc=1, device_id=(other, d), device_id_type=MESH)
    for other in (right, left):
        pl.semaphore_signal(barrier, inc=1, device_id=(me, other), device_id_type=MESH)

    lanes = 128
    lane_row = lax.broadcasted_iota(jnp.int32, (lanes, TILE), 0)
    lane_col = lax.broadcasted_iota(jnp.int32, (lanes, TILE), 1)
    apart = jnp.where(
        lane_row < 3 * heads, lax.rem(lane_row, heads) - lax.div(lane_col, P_SIZE), -heads
    )
    for tile in range(width // TILE):
        e4[:, tile * TILE : (tile + 1) * TILE] = jnp.where(
            apart == tile * (TILE // P_SIZE), 1.0, 0.0
        ).astype(BF16)

    def pack(value):
        hi, mid, lo = split3(value)
        lane = lax.broadcasted_iota(jnp.int32, value.shape, 1)
        hi, mid, lo = hi.astype(F32), mid.astype(F32), lo.astype(F32)
        chosen = jnp.where(lane < heads, hi, jnp.where(lane < 2 * heads, mid, lo))
        return jnp.where(lane < 3 * heads, chosen, 0.0).astype(BF16)

    rep = jnp.where(
        lax.rem(lax.broadcasted_iota(jnp.int32, (heads, lanes), 1), heads)
        == lax.broadcasted_iota(jnp.int32, (heads, lanes), 0),
        1.0,
        0.0,
    ).astype(BF16)
    mask = lax.broadcasted_iota(jnp.int32, (Q, Q), 0) >= lax.broadcasted_iota(jnp.int32, (Q, Q), 1)
    low = jnp.where(mask, 1.0, 0.0).astype(BF16)

    def turned(parts, right_mat):
        total = 0.0
        for one in parts:
            total = total + lax.dot_general(
                one, right_mat, (((0,), (0,)), ((), ())), preferred_element_type=F32
            )
        return total

    def gap(b):
        return slice(b % 2 * Q, (b % 2 + 1) * Q), slice(b // 2 * lanes, (b // 2 + 1) * lanes)

    fades = slice(blocks // 2 * lanes, blocks // 2 * lanes + part)
    kept = slice(width - gw, width)

    mids, tots = [], []
    for b in range(blocks):
        rows = slice(b * Q, (b + 1) * Q)
        ld4 = turned(split3(ld_ref[:, rows]), rep)
        step4 = turned(split3(step_ref[:, rows]), rep)
        parts = split3(ld4)
        cum = dot(low, parts[0]) + dot(low, parts[1]) + dot(low, parts[2])
        mid = cum[Q // 2 - 1 : Q // 2, :]
        gbuf[gap(b)] = cum - mid
        u4[rows, :] = pack(step4 * jnp.exp(mid - cum))
        mids.append(mid)
        tots.append(cum[Q - 1 : Q, :])
    row = lax.broadcasted_iota(jnp.int32, (blocks, lanes), 0)
    zero = jnp.zeros((blocks, lanes), F32)
    m8, t8, o8, s8 = zero, zero, zero, zero
    run = jnp.zeros((1, lanes), F32)
    for b in range(blocks):
        m8 = jnp.where(row == b, mids[b], m8)
        t8 = jnp.where(row == b, tots[b], t8)
        o8 = jnp.where(row == b, run, o8)
        run = run + tots[b]
    dl_pair[0] = jnp.broadcast_to(run, (8, lanes))
    later = jnp.zeros((1, lanes), F32)
    for b in reversed(range(blocks)):
        s8 = jnp.where(row == b, later, s8)
        later = later + tots[b]
    rt[...] = dot(pack(jnp.exp(s8 + t8 - m8)), e4[...])
    fac[...] = jnp.zeros((N, width), F32)
    taps_x[...] = 0.5 * cwx[...]
    for k in range(KCONV):
        for g in range(groups):
            taps_bc[k : k + 1, g * 2 * N : (g + 1) * 2 * N] = 0.5 * cwbc[k, g : g + 1, :]

    def halo(q):
        src = bc_hbm.at[pl.ds(length - LEAD, LEAD)]
        dst = bcr.at[pl.ds(0, LEAD)]
        if q < strips:
            src = x_hbm.at[pl.ds(length - LEAD, LEAD), pl.ds(q * piece, piece)]
            dst = rs_send.at[pl.ds(q * strip, LEAD)]
        return pltpu.make_async_remote_copy(
            src_ref=src,
            dst_ref=dst,
            send_sem=halo_send.at[q],
            recv_sem=halo_recv.at[q],
            device_id=(after, d),
            device_id_type=MESH,
        )

    def to_seq(src, dst, send, recv, slot, there, other):
        return pltpu.make_async_remote_copy(
            src_ref=src.at[slot],
            dst_ref=dst.at[there],
            send_sem=send.at[0],
            recv_sem=recv.at[0],
            device_id=(other, d),
            device_id_type=MESH,
        )

    def all_of(ref, sem):
        others = ref.at[pl.ds(0, chips - 1)]
        return pltpu.make_async_copy(others, others, sem.at[0])

    def to_sibling(src, dst, slot):
        return pltpu.make_async_remote_copy(
            src_ref=src,
            dst_ref=dst,
            send_sem=pair_s.at[slot],
            recv_sem=pair_r.at[slot],
            device_id=(sibling, d),
            device_id_type=MESH,
        )

    def decays():
        return to_sibling(dl_pair.at[0], dl_pair.at[1], 2)

    def states(slot):
        return to_sibling(pair_send.at[slot], pair_recv.at[slot], slot)

    def back(cp):
        cols = pl.ds(cp * part, part)
        return to_sibling(pair_send.at[1, :, cols], pair_recv.at[1, :, cols], 1 if cp == 0 else 2 + cp)

    def conv(buf, taps, r0, cols, tap_cols):
        prev = buf[pl.ds(r0, LEAD), cols].astype(F32)[LEAD - 8 :]
        cur = buf[pl.ds(r0 + LEAD, Q), cols].astype(F32)
        ext = jnp.concatenate([prev, cur], 0)
        total = taps[KCONV - 1 : KCONV, tap_cols] * cur
        for k in range(1, KCONV):
            total = total + taps[KCONV - 1 - k : KCONV - k, tap_cols] * pltpu.roll(ext, k, 0)[8:]
        return total * jnp.tanh(total) + total

    def of_group(g, tile):
        return pl.ds(pl.multiple_of(g * gw + tile * TILE, TILE), TILE)

    def convolve(g, b):
        r0 = pl.multiple_of(b * Q, Q)
        both = pl.ds(pl.multiple_of(g * 2 * N, 2 * N), 2 * N)
        bcb[pl.ds(r0, Q), both] = conv(bcr, taps_bc, r0, both, both).astype(BF16)
        for k in range(gw // CONV_COLS):
            cols = pl.ds(pl.multiple_of(g * gw + k * CONV_COLS, CONV_COLS), CONV_COLS)
            inside = slice(k * CONV_COLS % piece, k * CONV_COLS % piece + CONV_COLS)
            q = g * per_group + k * CONV_COLS // piece
            xc = conv(rs_send, taps_x, pl.multiple_of(r0 + q * strip, LEAD), inside, cols).astype(BF16)
            xb[pl.ds(r0, Q), cols] = xc
            ub[pl.ds(r0, Q), cols] = (
                xc.astype(F32) * dot(u4[pl.ds(r0, Q), :], e4[:, cols])
            ).astype(BF16)

    def gather(g, b):
        r0 = pl.multiple_of(b * Q, Q)
        b_turned = bcb[pl.ds(r0, Q), pl.ds(pl.multiple_of(g * 2 * N, 2 * N), N)].astype(F32).T.astype(BF16)
        for tile in range(gw // TILE):
            cols = of_group(g, tile)
            fresh = dot(b_turned, ub[pl.ds(r0, Q), cols])
            pst[b, :, cols] = fresh
            fac[:, cols] = fac[:, cols] + rt[pl.ds(b, 1), cols] * fresh

    load_bc.wait()
    for q in range(per_group):
        load_x((1 - core) * per_group + q).wait()

    lead_turn = blocks + blocks // 2 - 1

    def place(turn):
        sent = (turn < blocks - 1) | (turn == lead_turn)
        others = jnp.where(turn < lead_turn, 2 * blocks - 2 - turn, 2 * blocks - 1 - turn)
        return (
            jnp.where(sent, 1 - core, core),
            jnp.where(turn < blocks - 1, blocks - 1 - turn, jnp.where(turn == lead_turn, 0, others)),
        )

    def first_pass(turn, carry):
        @pl.when(turn == blocks - 1)
        def _():
            for q in range(per_group):
                load_x(core * per_group + q).wait()
            load_z.start()
            load_w(0).start()
            load_w(1).start()

        @pl.when(turn == blocks - 3)
        def _():
            pl.semaphore_wait(barrier, chips + 3)
            for q in range(strips + 1):
                halo(q).start()
            decays().start()

        @pl.when(turn == lead_turn)
        def _():
            for q in range(strips + 1):
                halo(q).wait_recv()

            @pl.when(me == 0)
            def _():
                for q in range(strips):
                    rs_send[q * strip : q * strip + LEAD, :] = jnp.zeros((LEAD, piece), BF16)
                bcr[:LEAD, :] = jnp.zeros((LEAD, bcr.shape[1]), BF16)

        gather(*place(turn - 1))
        convolve(*place(turn))

        @pl.when(turn == lead_turn + 1)
        def _():
            for tile in range(gw // TILE):
                pair_send[0, :, tile * TILE : (tile + 1) * TILE] = fac[
                    :, of_group(1 - core, tile)
                ].astype(BF16)
            states(0).start()

        return carry

    convolve(1 - core, blocks - 1)
    lax.fori_loop(1, 2 * blocks, first_pass, 0)
    gather(core, 0)

    decays().wait_recv()
    log_mine, log_other = dl_pair[0], dl_pair[1]
    first_core = core == 0
    of_core = pl.ds(pl.multiple_of(core * gw, gw), gw)
    fade_0 = dot(pack(jnp.exp(jnp.where(first_core, log_mine, log_other))), e4[:, of_core])
    fade_1 = dot(pack(jnp.exp(jnp.where(first_core, log_other, log_mine))), e4[:, of_core])
    fade_chip = pack(jnp.exp(log_mine + log_other)).astype(F32)
    fade_chip = jnp.concatenate([fade_chip, fade_chip], 0).astype(BF16)
    states(0).wait_recv()
    for rp in range(row_parts):
        for cp in range(col_parts):
            rows, cols = slice(rp * 16, (rp + 1) * 16), slice(cp * part, (cp + 1) * part)
            mine = fac[rows, pl.ds(pl.multiple_of(core * gw + cp * part, part), part)]
            other = pair_recv[0, rows, cols].astype(F32)
            state_0 = jnp.where(first_core, mine, other)
            state_1 = jnp.where(first_core, other, mine)
            faded = jnp.concatenate([fade_1[:, cols]] * 2, 0) * state_0
            gbuf[rows, width - gw + cp * part : width - gw + (cp + 1) * part] = state_0
            fmsg[rp * col_parts + cp, :, 0:part] = (faded + state_1).astype(BF16)
            fmsg[rp * col_parts + cp, :, part : part + lanes] = fade_chip

    def send_state(k, carry):
        j = lax.rem(chip + k, chips)
        to_seq(fmsg, frecv, f_s, f_r, j, chip, 2 * j + core).start()
        return carry

    lax.fori_loop(1, chips, send_state, 0, unroll=True)

    gbuf[N : N + 8, kept] = fade_0
    for ref, value in ((em, jnp.exp(m8)), (et, jnp.exp(t8 - m8)), (eo, jnp.exp(o8))):
        ref[...] = dot(pack(value), e4[...])
    parts = split3(jnp.broadcast_to(skip_ref[...], (8, heads)))
    skx[...] = dot(pack(dot(parts[0], rep) + dot(parts[1], rep) + dot(parts[2], rep)), e4[...])
    frecv_mine = fmsg[chip]
    for b in range(blocks):
        rows = slice(b * Q, (b + 1) * Q)
        a4[rows, :] = pack(jnp.exp(gbuf[gap(b)]))

    def recur(tile, carry):
        cols = pl.ds(pl.multiple_of(tile * 128, 128), 128)
        state = jnp.zeros((N, 128), F32)
        for b in range(blocks):
            fresh = pst[b, :, cols]
            pst[b, :, cols] = state
            state = et[b : b + 1, cols] * (fresh + em[b : b + 1, cols] * state)
        return carry

    lax.fori_loop(0, width // 128, recur, 0)

    all_of(frecv, f_r).wait()
    frecv[chip] = frecv_mine
    here = pl.multiple_of(core * gw + lax.rem(chip, col_parts) * part, part)
    arrived_fades = frecv[:, :, part : part + lanes].reshape(chips * 16, lanes)
    gbuf[: chips * 16, fades] = dot(arrived_fades, e4[:, pl.ds(here, part)])
    state = jnp.zeros((16, part), F32)
    for i in range(chips):
        imsg[i] = state.astype(BF16)
        state = gbuf[i * 16 : (i + 1) * 16, fades] * state + frecv[i, :, 0:part].astype(F32)

    def send_back(k, carry):
        j = lax.rem(chip + k, chips)
        to_seq(imsg, irecv, i_s, i_r, j, chip, 2 * j + core).start()
        return carry

    lax.fori_loop(1, chips, send_back, 0, unroll=True)
    irecv_mine = imsg[chip]
    all_of(irecv, i_r).wait()
    irecv[chip] = irecv_mine
    for cp in range(col_parts):
        for rp in range(row_parts):
            rows = slice(rp * 16, (rp + 1) * 16)
            cols = slice(width - gw + cp * part, width - gw + (cp + 1) * part)
            enters = irecv[rp * col_parts + cp].astype(F32)
            fade = gbuf[N : N + 8, cols]
            passed = jnp.concatenate([fade, fade], 0) * enters + gbuf[rows, cols]
            fac[rows, pl.ds(pl.multiple_of(core * gw + cp * part, part), part)] = jnp.where(
                first_core, enters, passed
            )
            pair_send[1, rows, cp * part : (cp + 1) * part] = jnp.where(
                first_core, passed, enters
            ).astype(BF16)
        back(cp).start()
    load_z.wait()
    load_w(0).wait()
    load_w(1).wait()

    for cp in range(col_parts):
        back(cp).wait_recv()
        for tile in range(cp * part // TILE, (cp + 1) * part // TILE):
            fac[:, of_group(1 - core, tile)] = pair_recv[1, :, tile * TILE : (tile + 1) * TILE].astype(F32)

    def second_pass(chunk):
        for g in range(groups):
            for i in range(chunk_rows // Q):
                b = chunk * (chunk_rows // Q) + i
                r0 = pl.multiple_of(b * Q, Q)
                b_mat = bcb[pl.ds(r0, Q), slice(g * 2 * N, g * 2 * N + N)]
                c_mat = bcb[pl.ds(r0, Q), g * 2 * N + N : (g + 1) * 2 * N]
                scores = lax.dot_general(
                    c_mat, b_mat, (((1,), (1,)), ((), ())), preferred_element_type=F32
                )
                lhs = jnp.concatenate([jnp.where(mask, scores, 0.0).astype(BF16), c_mat], 1)
                for tile in range(gw // TILE):
                    cols = slice(g * gw + tile * TILE, g * gw + (tile + 1) * TILE)
                    entering = em[pl.ds(b, 1), cols] * (
                        pst[b, :, cols] + eo[pl.ds(b, 1), cols] * fac[:, cols]
                    )
                    rhs = jnp.concatenate([ub[pl.ds(r0, Q), cols], entering.astype(BF16)], 0)
                    y = dot(a4[pl.ds(r0, Q), :], e4[:, cols]) * dot(lhs, rhs)
                    y = y + skx[0:1, cols] * xb[pl.ds(r0, Q), cols].astype(F32)
                    z_half = 0.5 * zb[pl.ds(r0, Q), cols].astype(F32)
                    gbuf[i * Q : (i + 1) * Q, cols] = y * (z_half * jnp.tanh(z_half) + z_half)
        for i in range(chunk_rows // Q):
            r0 = pl.multiple_of((chunk * (chunk_rows // Q) + i) * Q, Q)
            for g in range(groups):
                squares = jnp.zeros((Q, 128), F32)
                for k in range(gw // 128):
                    gated = gbuf[i * Q : (i + 1) * Q, g * gw + k * 128 : g * gw + (k + 1) * 128]
                    squares = squares + gated * gated
                mean = jnp.sum(squares, axis=1, keepdims=True) * (1.0 / gw)
                scale = lax.rsqrt(mean + EPS)
                for tile in range(gw // TILE):
                    cols = slice(g * gw + tile * TILE, g * gw + (tile + 1) * TILE)
                    ub[pl.ds(r0, Q), cols] = (
                        gbuf[i * Q : (i + 1) * Q, cols] * scale * gain_ref[:, cols]
                    ).astype(BF16)

    def product(way, p, chunk):
        first = pl.multiple_of(way * half + p * piece, piece)
        rows = pl.ds(pl.multiple_of(chunk * chunk_rows, chunk_rows), chunk_rows)
        return dot(ub[rows, :], wb[:, pl.ds(first, piece)])

    def outgoing(way, turn, p):
        index = (lax.rem(turn, 2) * 2 + way) * PIECES + p
        return pl.ds(pl.multiple_of(index * chunk_rows, chunk_rows), chunk_rows)

    def hop(way, turn, p):
        return pltpu.make_async_remote_copy(
            src_ref=rs_send.at[outgoing(way, turn, p)],
            dst_ref=rs_recv.at[way, turn, p],
            send_sem=r_s.at[way, turn, p],
            recv_sem=r_r.at[way, turn, p],
            device_id=(me, jnp.where(way == 0, right, left)),
            device_id_type=MESH,
        )

    def stage(way, turn, p):
        chunk = lax.rem(jnp.where(way == 0, d + 2 * HEADS - 1 - turn, d + 1 + turn), HEADS)
        total = product(way, p, chunk)
        if not (isinstance(turn, int) and turn == 0):

            @pl.when(turn == 2)
            def _():
                hop(way, 0, p).wait_send()

            hop(way, turn - 1, p).wait_recv()
            total = total + rs_recv[way, turn - 1, p].astype(F32)
        rs_send[outgoing(way, turn, p), :] = total.astype(BF16)
        hop(way, turn, p).start()

    def first_stages(k, carry):
        @pl.when(k < 2)
        def _():
            second_pass(jnp.where(k == 0, left, right))

        stage(lax.rem(k, 2), 0, lax.div(k, 2))
        return carry

    lax.fori_loop(0, 2 * PIECES, first_stages, 0)

    def later_stages(k, carry):
        turn = 1 + lax.div(k, 2 * PIECES)
        q = lax.rem(k, 2 * PIECES)

        @pl.when(q == 0)
        def _():
            second_pass(lax.rem(jnp.where(turn == 1, d + 2, d), HEADS))

        stage(lax.rem(q, 2), turn, lax.div(q, 2))
        return carry

    lax.fori_loop(0, (HEADS - 2) * 2 * PIECES, later_stages, 0)

    def own(q, carry):
        total = product(lax.rem(q, 2), lax.div(q, 2), d)
        pst[q, :, 0:piece] = total[:Q]
        pst[q, :, piece : 2 * piece] = total[Q:]
        return carry

    lax.fori_loop(0, 2 * PIECES, own, 0)

    def to_out(way, p):
        first = pl.multiple_of(way * half + p * piece, piece)
        return pltpu.make_async_copy(
            zb.at[
                pl.ds(pl.multiple_of(way * chunk_rows, chunk_rows), chunk_rows),
                pl.ds(pl.multiple_of(p * piece, piece), piece),
            ],
            out_hbm.at[:, pl.ds(first, piece)],
            out_sem.at[way, p],
        )

    def finish(q, carry):
        way, p = lax.rem(q, 2), lax.div(q, 2)
        hop(way, HEADS - 2, p).wait_recv()
        arrived = rs_recv[way, HEADS - 2, p].astype(F32)
        cols = pl.ds(pl.multiple_of(p * piece, piece), piece)
        base = pl.multiple_of(way * chunk_rows, chunk_rows)
        zb[pl.ds(base, Q), cols] = (pst[q, :, 0:piece] + arrived[:Q]).astype(BF16)
        zb[pl.ds(base + Q, Q), cols] = (pst[q, :, piece : 2 * piece] + arrived[Q:]).astype(BF16)
        to_out(way, p).start()
        return carry

    lax.fori_loop(0, 2 * PIECES, finish, 0)

    for q in range(strips + 1):
        halo(q).wait_send()
    decays().wait_send()
    states(0).wait_send()
    for cp in range(col_parts):
        back(cp).wait_send()
    all_of(fmsg, f_s).wait()
    all_of(imsg, i_s).wait()

    def await_ring(q, carry):
        way, p = lax.rem(q, 2), lax.div(q, 2)
        for turn in range(1, HEADS - 1):
            hop(way, turn, p).wait_send()
        to_out(way, p).wait()
        return carry

    lax.fori_loop(0, 2 * PIECES, await_ring, 0)


def local(
    x_input,
    z_input,
    bc_input,
    conv_weight_x,
    conv_weight_bc,
    step_size,
    log_decay,
    skip_gain,
    norm_gain,
    out_weight,
):
    ns = lax.axis_size("seq")
    length, width = x_input.shape
    groups = bc_input.shape[1]
    columns = out_weight.shape[1]
    blocks = length // Q
    heads = step_size.shape[1]
    chips = ns // 2
    part = width // groups // (chips // (N // 16))
    piece = columns // 2 // PIECES
    rows = length // HEADS
    any_space = pl.BlockSpec(memory_space=pl.ANY)
    vmem = pl.BlockSpec(memory_space=pltpu.VMEM)
    dma = pltpu.SemaphoreType.DMA
    return pl.pallas_call(
        functools.partial(kernel, ns),
        out_shape=jax.ShapeDtypeStruct((rows, columns), BF16),
        in_specs=[any_space] * 4 + [vmem] * 6,
        out_specs=any_space,
        scratch_shapes=[
            pltpu.VMEM((length, width), BF16),
            pltpu.VMEM((length, width), BF16),
            pltpu.VMEM((LEAD + length, groups * 2 * N), BF16),
            pltpu.VMEM((length, groups * 2 * N), BF16),
            pltpu.VMEM((width, columns), BF16),
            pltpu.VMEM((length, width), BF16),
            pltpu.VMEM((blocks, N, width), F32),
            pltpu.VMEM((N, width), F32),
            pltpu.VMEM((128, width), BF16),
            pltpu.VMEM((length, 128), BF16),
            pltpu.VMEM((length, 128), BF16),
            pltpu.VMEM((blocks, width), F32),
            pltpu.VMEM((blocks, width), F32),
            pltpu.VMEM((blocks, width), F32),
            pltpu.VMEM((blocks, width), F32),
            pltpu.VMEM((8, width), F32),
            pltpu.VMEM((KCONV, width), F32),
            pltpu.VMEM((KCONV, groups * 2 * N), F32),
            pltpu.VMEM((2, 8, 128), F32),
            pltpu.VMEM((2, N, width // groups), BF16),
            pltpu.VMEM((2, N, width // groups), BF16),
            pltpu.VMEM((chips, 16, part + 128), BF16),
            pltpu.VMEM((chips, 16, part + 128), BF16),
            pltpu.VMEM((chips, 16, part), BF16),
            pltpu.VMEM((chips, 16, part), BF16),
            pltpu.VMEM((rows, width), F32),
            pltpu.VMEM((max(4 * PIECES * rows, width // piece * (LEAD + length)), piece), BF16),
            pltpu.VMEM((2, HEADS - 1, PIECES, rows, piece), BF16),
            dma((width // piece + 4,)),
            dma((width // piece + 1,)),
            dma((width // piece + 1,)),
            dma((2 + chips // (N // 16),)),
            dma((2 + chips // (N // 16),)),
            dma((1,)),
            dma((1,)),
            dma((1,)),
            dma((1,)),
            dma((2, HEADS - 1, PIECES)),
            dma((2, HEADS - 1, PIECES)),
            dma((2, PIECES)),
        ],
        compiler_params=pltpu.CompilerParams(
            collective_id=0, has_side_effects=True, vmem_limit_bytes=60 * 2**20
        ),
        cost_estimate=pl.CostEstimate(
            flops=2 * length * width * columns,
            bytes_accessed=2 * (2 * length * width + width * columns),
            transcendentals=2 * length * width,
        ),
    )(
        x_input,
        z_input,
        bc_input.reshape(length, groups * 2 * N),
        out_weight,
        conv_weight_x,
        conv_weight_bc,
        step_size.T,
        log_decay.T,
        skip_gain.reshape(1, heads),
        norm_gain.reshape(1, width),
    )


def solution(mesh):
    in_specs = (
        P("seq", "head"),
        P("seq", "head"),
        P("seq", "head", None),
        P(None, "head"),
        P(None, "head", None),
        P("seq", "head"),
        P("seq", "head"),
        P("head"),
        P("head"),
        P("head", None),
    )
    out_specs = P(("seq", "head"), None)
    return jax.shard_map(local, mesh=mesh, in_specs=in_specs, out_specs=out_specs, check_vma=False)
```
